32 devices in a mesh: det: 4 (over z), tm: 8 (over y, x, core).
Axes of the slice: x: 2, y: 2, z: 4, core: 2. Of those that a mesh axis runs over, the one named last changes fastest.
Arguments:
- iterate: float32 [16, 262144], P(None, ('det', 'tm')), may hold values from -6 to 6
- residual: float32 [16, 262144], P(None, ('det', 'tm')), may hold values from -40 to 40
- direction: float32 [16, 262144], P(None, ('det', 'tm')), may hold values from -2.5 to 2.5
- precond: float32 [262144], P(('det', 'tm')), may hold values from 0.02 to 0.12
- patch_ids: int32 [128, 64], P('det', 'tm'), may hold values from 0 to 4095, as said below
- pixel_in: int32 [128, 8192], P('det', 'tm'), may hold values from 0 to 63
- weights: float32 [128, 8192], P('det', 'tm'), may hold values from 0.5 to 1.5
- filter_diag: float32 [128], P('det'), may hold values from 1 to 1.5
- filter_band: float32 [128, 64], P('det'), may hold values from 0.003125 to 0.0075
Outputs:
- new_iterate: float32 [16, 262144], P(None, ('det', 'tm'))
- new_residual: float32 [16, 262144], P(None, ('det', 'tm'))
- new_direction: float32 [16, 262144], P(None, ('det', 'tm'))
The draws below stay inside these ranges and needn't reach their ends.
Inputs may be any that keep to these rules, and one draw needn't show every extreme that they name: `patch_ids`: the blocks of one device (detectors 32 d0 .. and time blocks 8 t0 .. of its det index a and tm index c) name, for every owner o = a2 * 8 + c2, exactly 8 patches p with p // 128 = o.
All inputs are finite; a program needn't handle non-finite values.
Results may differ from the reference program's by a relative error of at most 0.0003.
Values sent between devices are 32-bit elements; how exact they have to be, the bound alone decides.
A program may use at most 64 MiB of HBM per device.

```python
import math
import jax
import jax.numpy as jnp
from jax import lax

PROBES = 16
SB = 128
PX = 64
ND_DEV = 32
PATCH_DEV = 128
H = 64
TB_DEV = 8
BLK_DEV = 256
PER_OWNER = 8
DGROUPS = 4
SPANS = 8
DETS = 128
TSAMP = 8192
TBLK = 64
NPIX = 262144
DEVICES = 32


def rising_field(key, level, limit):
    position = jnp.arange(NPIX, dtype=jnp.float32) / NPIX
    values = jax.random.normal(key, (PROBES, NPIX), jnp.float32) * level * (1.0 + position)[None, :]
    return jnp.clip(values, -limit, limit)


def draw_residual(key, part):
    return rising_field(jax.random.fold_in(key, 11), 4.0, 40.0)


def draw_direction(key, part):
    return rising_field(jax.random.fold_in(key, 23), 0.25, 2.5)


def draw_patch_ids(key, part):

    def one_device(device_index):
        dev_key = jax.random.fold_in(key, device_index)
        perm_key, off_key = jax.random.split(dev_key)
        owners = jnp.arange(BLK_DEV, dtype=jnp.int32) // PER_OWNER
        owners = jax.random.permutation(perm_key, owners)
        offset = jax.random.randint(off_key, (BLK_DEV,), 0, PATCH_DEV, dtype=jnp.int32)
        return owners * PATCH_DEV + offset
    blocks_all = jax.vmap(one_device)(jnp.arange(DEVICES, dtype=jnp.int32))
    blocks_all = blocks_all.reshape(DGROUPS, SPANS, ND_DEV, TB_DEV).transpose(0, 2, 1, 3)
    return blocks_all.reshape(DETS, TBLK).astype(jnp.int32)


def touch_ends(drawn, key, smallest, high):
    extent = drawn.shape
    place = [jax.random.randint(jax.random.fold_in(key, axis), (), 0, extent[axis]) for axis in range(len(extent))]
    drawn = drawn.at[tuple(place)].set(smallest)
    longest = extent.index(max(extent))
    place[longest] = (place[longest] + 1) % extent[longest]
    return drawn.at[tuple(place)].set(high)


def levels(rng, extent, pieces, low, top_value):
    factor_of = 1.0
    for axis_at, parts in pieces:
        heights = jax.random.uniform(jax.random.fold_in(jax.random.fold_in(rng, 6), axis_at), (parts,), jnp.float32, low / len(pieces), top_value / len(pieces))
        factor_of = factor_of * jnp.repeat(jnp.exp(heights), extent[axis_at] // parts).reshape((-1,) + (1,) * (len(extent) - 1 - axis_at))
    return factor_of


def gaussian(stream_key, shape, deviation, bound, pieces=(), held_as=jnp.bfloat16):
    gain = levels(stream_key, shape, pieces, -0.22, 0.18) if pieces else 1.0
    array = jax.random.normal(stream_key, shape, jnp.float32) * deviation * gain
    return jnp.minimum(jnp.maximum(array, -bound), bound).astype(held_as)


def setup_inputs(seed: int = 0) -> dict:
    keys = jax.random.split(jax.random.key(seed), 10)
    iterate = gaussian(keys[0], (PROBES, NPIX), 1.0, 6.0, ((1, 32),), jnp.float32)
    residual = draw_residual(jax.random.fold_in(keys[9], 71), 0)
    direction = draw_direction(jax.random.fold_in(keys[9], 71), 0)
    precond = jnp.clip(jnp.exp(math.log(0.12) - 1.7917595 * jax.random.uniform(keys[3], (NPIX,), jnp.float32) ** levels(keys[3], (NPIX,), ((0, 32),), -0.2, 0.2)), 0.02, 0.12)
    patch_ids = draw_patch_ids(jax.random.fold_in(keys[9], 71), 0)
    pixel_in = touch_ends(jax.random.randint(keys[5], (DETS, TSAMP), 0, PX), jax.random.fold_in(keys[5], 1), 0, PX - 1).astype(jnp.int32)
    weights = jnp.clip(0.5 + 1.0 * jax.random.uniform(keys[6], (DETS, TSAMP), jnp.float32) ** levels(keys[6], (DETS, TSAMP), ((0, 4), (1, 8)), -0.2, 0.2), 0.5, 1.5)
    filter_diag = jnp.clip(1.0 + 0.5 * jax.random.uniform(keys[7], (DETS,), jnp.float32) ** levels(keys[7], (DETS,), ((0, 4),), -0.2, 0.2), 1.0, 1.5)
    filter_band = jnp.clip(0.003125 + 0.004374999785795808 * jax.random.uniform(keys[8], (DETS, H), jnp.float32) ** levels(keys[8], (DETS, H), ((0, 4),), -0.2, 0.2), 0.003125, 0.0075)
    return dict(iterate=iterate, residual=residual, direction=direction, precond=precond, patch_ids=patch_ids, pixel_in=pixel_in, weights=weights, filter_diag=filter_diag, filter_band=filter_band)


def toeplitz_blocks(filter_diag, filter_band):
    half_band = filter_band.shape[1]
    block_len = 2 * half_band
    coeffs = jnp.concatenate([filter_diag[:, None], filter_band], axis=1)
    offsets = jnp.abs(jnp.arange(2 * block_len, dtype=jnp.int32)[:, None] - jnp.arange(block_len, dtype=jnp.int32)[None, :] - half_band)
    band_hot = (offsets[:, :, None] == jnp.arange(half_band + 1, dtype=jnp.int32)[None, None, :]).astype(jnp.float32)
    return jnp.einsum('usk,dk->dus', band_hot, coeffs, precision=lax.Precision.HIGHEST)


def reference(iterate, residual, direction, precond, patch_ids, pixel_in, weights, filter_diag, filter_band):
    norm_old = jnp.sum(residual * precond * residual, axis=1)
    toeplitz = toeplitz_blocks(filter_diag, filter_band)
    patch_groups = patch_ids.reshape(DGROUPS, ND_DEV, TBLK)
    pixel_groups = pixel_in.reshape(DGROUPS, ND_DEV, TSAMP)
    gain_groups = weights.reshape(DGROUPS, ND_DEV, TSAMP)
    toep_groups = toeplitz.reshape(DGROUPS, ND_DEV, 2 * SB, SB)

    def one_group(image_map, inputs):
        patch_rows, pixel_rows, gain_rows, toep_rows = inputs
        global_px = (jnp.repeat(patch_rows, SB, axis=1) * PX + pixel_rows).astype(jnp.int32)
        timeline = direction[:, global_px] * gain_rows[None]
        padded = jnp.pad(timeline, ((0, 0), (0, 0), (H, H)))
        windows = jnp.concatenate([
            padded[:, :, :TSAMP].reshape(PROBES, ND_DEV, TBLK, SB),
            padded[:, :, SB:TSAMP + SB].reshape(PROBES, ND_DEV, TBLK, SB)], axis=3)
        filtered = jnp.einsum('pdju,dus->pdjs', windows, toep_rows, precision=lax.Precision.HIGHEST)
        weighted = filtered.reshape(PROBES, ND_DEV, TSAMP) * gain_rows[None]
        added = jax.ops.segment_sum(weighted.reshape(PROBES, -1).T, global_px.reshape(-1), num_segments=NPIX).T
        return image_map + added, jnp.zeros((), jnp.float32)

    image_map = lax.scan(one_group, jnp.zeros((PROBES, NPIX), jnp.float32), (patch_groups, pixel_groups, gain_groups, toep_groups))[0]
    curvature = jnp.sum(direction * image_map, axis=1)
    step_size = norm_old / curvature
    new_iterate = iterate + step_size[:, None] * direction
    new_residual = residual - step_size[:, None] * image_map
    scaled = precond * new_residual
    norm_new = jnp.sum(new_residual * scaled, axis=1)
    new_direction = scaled + (norm_new / norm_old)[:, None] * direction
    return (new_iterate, new_residual, new_direction)
```

```python
import functools
import math

import jax
import jax.numpy as jnp
from jax import lax
from jax.experimental import pallas as pl
from jax.experimental.pallas import tpu as pltpu
from jax.sharding import PartitionSpec as P

PX = 64
MESH = pl.DeviceIdType.MESH


def halves(values):
    top = values.astype(jnp.bfloat16)
    return top, (values - top.astype(jnp.float32)).astype(jnp.bfloat16)


def vmem(count):
    return [pl.BlockSpec(memory_space=pltpu.VMEM)] * count


def smem(count):
    return [pl.BlockSpec(memory_space=pltpu.SMEM)] * count


def peers_of(spans, devices):
    me = lax.axis_index("det") * spans + lax.axis_index("tm")
    stride = spans + 1 if math.gcd(spans + 1, devices) == 1 else 1

    def ahead(step):
        return lax.rem(me + step * stride, devices)

    def behind(step):
        return lax.rem(me + (devices - step) * stride, devices)

    def place(peer):
        return (peer // spans, lax.rem(peer, spans))

    return me, ahead, behind, place


def remote(src, dst, sent, got, device):
    return pltpu.make_async_remote_copy(
        src_ref=src, dst_ref=dst, send_sem=sent, recv_sem=got, device_id=device, device_id_type=MESH
    )


def step_kernel(
    spans, devices,
    slot_ref, block_ref, diag_ref, ask_ref, way_ref, old_ref, scale_ref, pixel_ref, gain_ref, band_ref,
    image_ref, factor_ref,
    asked, numbers, table, served, patches, pixels, turned, gains, turned_gains, line, bands, hot,
    head, tail, before, after, cells, part, collected, spread, image, sums, held,
    ask_sent, ask_got, sent, got, local, edge_sent, edge_got, back_sent, back_got, sum_sent, sum_got,
):
    me, ahead, behind, place = peers_of(spans, devices)
    span, group = lax.axis_index("tm"), lax.axis_index("det")
    rows = pixel_ref.shape[0]
    blocks = block_ref.shape[0]
    per_row = blocks // rows
    per_owner = blocks // devices
    pairs = per_owner // 2
    half = rows // 2
    tiles = way_ref.shape[1] // 128
    deep = pairs * 8
    left = lax.broadcasted_iota(jnp.int32, (8, 128), 1) < 64

    barrier = pltpu.get_barrier_semaphore()

    @pl.loop(1, devices)
    def _(step):
        pl.semaphore_signal(barrier, inc=1, device_id=place(ahead(step)), device_id_type=MESH)

    @pl.loop(0, tiles, unroll=2)
    def _(q):
        for h in range(2):
            tile = way_ref[8 * h : 8 * h + 8, pl.ds(pl.multiple_of(q * 128, 128), 128)]
            table[0, h, q] = tile
            table[1, h, q] = pltpu.roll(tile, 64, 1)

    pl.semaphore_wait(barrier, devices - 1)

    def ask(step, slot):
        peer = ahead(step)
        return remote(
            ask_ref.at[peer], asked.at[slot], ask_sent.at[step], ask_got.at[step], place(peer)
        )

    def give(h, step, slot):
        peer = ahead(step)
        return remote(
            served.at[h, peer], patches.at[h, slot], sent.at[h, step], got.at[h, step], place(peer)
        )

    @pl.loop(1, devices)
    def _(step):
        ask(step, me).start()

    asked[me] = ask_ref[me]

    for r in range(0, rows, 8):
        for j in range(per_row):
            these = pl.ds(r * per_row + j, 8, stride=per_row)
            pixel = pixel_ref[r : r + 8, 128 * j : 128 * j + 128]
            gain = gain_ref[r : r + 8, 128 * j : 128 * j + 128]
            pixels[these, :] = pixel
            turned[these, :] = pltpu.roll(pixel, 64, 1)
            gains[these, :] = gain
            turned_gains[these, :] = pltpu.roll(gain, 64, 1)

    @pl.loop(1, devices)
    def _(step):
        ask(step, behind(step)).wait_recv()

    move = pltpu.make_async_copy(asked, numbers, local)
    move.start()
    move.wait()

    def serve(h, peer, dst):
        for i in range(pairs):
            a, b = numbers[peer, 0, 2 * i], numbers[peer, 0, 2 * i + 1]
            dst[h, peer, i] = jnp.where(left, table[a & 1, h, a >> 1], table[1 - (b & 1), h, b >> 1])

    for h in range(2):

        @pl.loop(1, devices)
        def _(step):
            serve(h, ahead(step), served)
            give(h, step, me).start()

        serve(h, me, patches)

    lane = lax.broadcasted_iota(jnp.int32, (1, 128), 1)
    band = jnp.concatenate([band_ref[...], jnp.zeros((rows, 128 - band_ref.shape[1]), jnp.float32)], axis=1)
    wanted = jnp.broadcast_to(jnp.where(lane < 64, 63 - lane, jnp.maximum(lane - 65, 0)), (rows, 128))
    upper = jnp.take_along_axis(band, wanted, axis=1)
    lower = jnp.where(
        lane == 0, jnp.take_along_axis(band, jnp.full((rows, 128), 63, jnp.int32), axis=1), 0.0
    )
    sums[...] = jnp.zeros_like(sums)
    cells_of_band = jnp.concatenate([lower, upper], axis=1)
    held_bands = cells_of_band

    wide_lane = lax.broadcasted_iota(jnp.int32, (1, 256), 1)
    for d in range(rows):
        base = jnp.where(wide_lane == 192, diag_ref[d], held_bands[d : d + 1])
        around = pltpu.roll(jnp.broadcast_to(base, (128, 256)), 0, 1, stride=1, stride_axis=0)
        bands[d] = jnp.concatenate(
            [
                jnp.concatenate(halves(around[:, :128]), axis=1),
                jnp.concatenate(halves(around[:, 128:]), axis=1),
            ],
            axis=0,
        )

    spot = lax.broadcasted_iota(jnp.int32, (PX, 128), 0)

    @pl.loop(0, blocks, unroll=2)
    def _(s):
        pixel = jnp.broadcast_to(pixels[pl.ds(block_ref[s], 1), :], (PX, 128))
        hot[s] = jnp.where(spot == pixel, 1.0, 0.0).astype(jnp.bfloat16)

    asks = asked[:, 0, :]
    even = jnp.concatenate(
        [jnp.broadcast_to(asks[:, 2 * i : 2 * i + 1], (devices, 2 * tiles)) for i in range(pairs)], axis=0
    )
    odd = jnp.concatenate(
        [jnp.broadcast_to(asks[:, 2 * i + 1 : 2 * i + 2], (devices, 2 * tiles)) for i in range(pairs)], axis=0
    )
    column = lax.broadcasted_iota(jnp.int32, even.shape, 1)
    first = column < tiles
    target = jnp.where(first, 2 * column, 2 * (column - tiles) + 1)
    straight = jnp.where(jnp.where(first, even, odd) == target, 1.0, 0.0)
    crossed = jnp.where(jnp.where(first, odd, even) == target, 1.0, 0.0)
    spread[...] = jnp.concatenate([straight.T, crossed.T], axis=1).astype(jnp.bfloat16)

    def scan(h, peer):
        for i in range(pairs):
            patch = patches[h, peer, i]
            for side in range(2):
                s = peer * per_owner + 2 * i + side
                b = block_ref[s]
                pixel = jnp.broadcast_to(turned[pl.ds(b, 1), :], (8, 128)) + 64 * side
                gain = jnp.broadcast_to(turned_gains[pl.ds(b, 1), :], (8, 128))
                line[h, s] = jnp.take_along_axis(patch, pixel, axis=1) * gain

    def arrive(h, low, high):
        @pl.loop(low, high)
        def _(step):
            give(h, step, behind(step)).wait_recv()
            scan(h, behind(step))

    forth = [
        remote(tail.at[h], before.at[h], edge_sent.at[h, 0], edge_got.at[h, 0],
               (group, lax.rem(span + 1, spans)))
        for h in range(2)
    ]
    back = [
        remote(head.at[h], after.at[h], edge_sent.at[h, 1], edge_got.at[h, 1],
               (group, lax.rem(span + spans - 1, spans)))
        for h in range(2)
    ]

    def edges(h):
        @pl.loop(0, half)
        def _(d):
            start, end = d * per_row, d * per_row + per_row - 1
            far = half * per_row
            head[h, d] = jnp.where(
                left, pltpu.roll(line[h, slot_ref[start]], 64, 1), line[h, slot_ref[start + far]]
            )
            tail[h, d] = jnp.where(
                left, line[h, slot_ref[end]], pltpu.roll(line[h, slot_ref[end + far]], 64, 1)
            )

        forth[h].start()
        back[h].start()

    def edges_in(h):
        forth[h].wait()
        back[h].wait()

        @pl.when(span == 0)
        def _():
            before[h] = jnp.zeros_like(before[h])

        @pl.when(span == spans - 1)
        def _():
            after[h] = jnp.zeros_like(after[h])

    def one_row(h, d, early, late):
        mine = [early] + [line[h, slot_ref[d * per_row + j]] for j in range(per_row)] + [late]
        shifted = [jnp.where(left, mine[m], mine[m + 1]) for m in range(per_row + 1)]
        near = jnp.concatenate(shifted[:-1], axis=0)
        far = jnp.concatenate(shifted[1:], axis=0)
        wide = jnp.concatenate(
            [jnp.concatenate(halves(near), axis=0), jnp.concatenate(halves(far), axis=0)], axis=1
        )
        made = jnp.dot(wide, bands[d], preferred_element_type=jnp.float32)
        n = 8 * per_row
        filtered = made[:n, :128] + (made[n:, :128] + made[:n, 128:])
        for j in range(per_row):
            gain = jnp.broadcast_to(gains[pl.ds(d * per_row + j, 1), :], (8, 128))
            values = filtered[8 * j : 8 * j + 8] * gain
            top = values.astype(jnp.bfloat16).astype(jnp.float32)
            cells[h, d * per_row + j] = jnp.concatenate([top, values - top], axis=0).astype(jnp.bfloat16)

    def filter_all(h):
        @pl.loop(0, half)
        def _(d):
            early, late = before[h, d], after[h, d]
            one_row(h, d, early, pltpu.roll(late, 64, 1))
            one_row(h, d + half, pltpu.roll(early, 64, 1), late)

    blank = jnp.zeros((PX, 128), jnp.bfloat16)

    def project(h, peer, dst, where):
        for i in range(pairs):
            s = peer * per_owner + 2 * i
            both = jnp.concatenate([cells[h, block_ref[s]], cells[h, block_ref[s + 1]]], axis=1)
            grid = jnp.concatenate(
                [
                    jnp.concatenate([hot[s], blank], axis=1),
                    jnp.concatenate([blank, hot[s + 1]], axis=1),
                ],
                axis=0,
            )
            added = lax.dot_general(
                both, grid, (((1,), (1,)), ((), ())), preferred_element_type=jnp.float32
            )
            dst[pl.ds(pl.multiple_of(where + 8 * i, 8), 8), :] = added[:8] + added[8:]

    def rows_of(h, slot):
        return pl.ds(pl.multiple_of((h * devices + slot) * deep, 8), deep)

    def send_back(h, step, slot):
        peer = ahead(step)
        return remote(
            part.at[rows_of(h, peer)], collected.at[rows_of(h, slot)],
            back_sent.at[h, step], back_got.at[h, step], place(peer),
        )

    def project_all(h):
        @pl.loop(1, devices)
        def _(step):
            peer = ahead(step)
            project(h, peer, part, (h * devices + peer) * deep)
            send_back(h, step, me).start()

        project(h, me, collected, (h * devices + me) * deep)

    def gather_up(h):
        @pl.loop(1, devices)
        def _(step):
            send_back(h, step, behind(step)).wait_recv()

        wide_left = lax.broadcasted_iota(jnp.int32, (tiles, 128), 1) < 64
        for k in range(8):
            came = jnp.concatenate(
                [
                    collected[pl.ds(h * devices * deep + 8 * i + k, devices, stride=deep), :]
                    for i in range(pairs)
                ],
                axis=0,
            )
            came = jnp.concatenate([came, pltpu.roll(came, 64, 1)], axis=0)
            total = jnp.dot(
                spread[...], jnp.concatenate(halves(came), axis=1), preferred_element_type=jnp.float32
            )
            total = total[:, :128] + total[:, 128:]
            image[pl.ds(h * tiles * 8 + k, tiles, stride=8), :] = jnp.where(
                wide_left, total[:tiles], total[tiles:]
            )

        zero = jnp.zeros((8, 128), jnp.float32)

        def add(q, totals):
            these = pl.ds(pl.multiple_of(q * 128, 128), 128)
            tile = image[pl.ds(pl.multiple_of((h * tiles + q) * 8, 8), 8), :]
            image_ref[8 * h : 8 * h + 8, these] = tile
            old = old_ref[8 * h : 8 * h + 8, these]
            scale = jnp.broadcast_to(scale_ref[:, these], (8, 128))
            way = way_ref[8 * h : 8 * h + 8, these]
            lean = scale * old
            return (
                totals[0] + old * lean,
                totals[1] + way * tile,
                totals[2] + tile * lean,
                totals[3] + tile * (scale * tile),
            )

        totals = lax.fori_loop(0, tiles, add, (zero,) * 4, unroll=4)
        whole = sums[...]
        lanes = lax.broadcasted_iota(jnp.int32, (8, 128), 1)
        for i, total in enumerate(totals):
            whole = jnp.where(lanes == 4 * h + i, jnp.sum(total, axis=1, keepdims=True), whole)
        sums[...] = whole

    scan(0, me)
    arrive(0, 1, devices)
    edges(0)
    scan(1, me)
    arrive(1, 1, devices // 2)
    edges_in(0)
    filter_all(0)
    arrive(1, devices // 2, devices)
    edges(1)
    project_all(0)
    edges_in(1)
    filter_all(1)
    project_all(1)

    @pl.loop(1, devices)
    def _(step):
        ask(step, me).wait_send()
        give(0, step, me).wait_send()
        give(1, step, me).wait_send()

    gather_up(0)
    gather_up(1)

    def give_sums(step, slot):
        return remote(sums, held.at[slot], sum_sent.at[step], sum_got.at[step], place(ahead(step)))

    @pl.loop(1, devices)
    def _(step):
        give_sums(step, me).start()

    held[me] = sums[...]

    @pl.loop(1, devices)
    def _(step):
        send_back(0, step, me).wait_send()
        send_back(1, step, me).wait_send()
        give_sums(step, me).wait_send()
        give_sums(step, behind(step)).wait_recv()

    total = jnp.sum(held[...], axis=0)
    for h in range(2):
        norm_old, curvature, cross, square = (total[:, 4 * h + i : 4 * h + i + 1] for i in range(4))
        step_size = norm_old / curvature
        norm_new = norm_old - step_size * (2.0 * cross - step_size * square)
        lanes = lax.broadcasted_iota(jnp.int32, (8, 128), 1)
        factor_ref[8 * h : 8 * h + 8, :] = jnp.where(lanes == 0, step_size, norm_new / norm_old)


def one_step(slot, block, diag, ask, way, old, scale, pixels, gains, band, spans, devices):
    blocks = slot.shape[0]
    rows = pixels.shape[0]
    per_owner = blocks // devices
    pairs = per_owner // 2
    tiles = way.shape[1] // 128
    edge = (2, rows // 2, 8, 128)
    both = (2, devices, pairs, 8, 128)
    flat = (2 * devices * pairs * 8, 128)
    dma = pltpu.SemaphoreType.DMA
    return pl.pallas_call(
        functools.partial(step_kernel, spans, devices),
        out_shape=(
            jax.ShapeDtypeStruct(way.shape, jnp.float32),
            jax.ShapeDtypeStruct((way.shape[0], 128), jnp.float32),
        ),
        in_specs=smem(3) + vmem(7),
        out_specs=tuple(vmem(2)),
        scratch_shapes=[
            pltpu.VMEM(ask.shape, jnp.int32),
            pltpu.SMEM(ask.shape, jnp.int32),
            pltpu.VMEM((2, 2, tiles, 8, 128), jnp.float32),
            pltpu.VMEM(both, jnp.float32),
            pltpu.VMEM(both, jnp.float32),
            pltpu.VMEM((blocks, 128), jnp.int32),
            pltpu.VMEM((blocks, 128), jnp.int32),
            pltpu.VMEM((blocks, 128), jnp.float32),
            pltpu.VMEM((blocks, 128), jnp.float32),
            pltpu.VMEM((2, blocks, 8, 128), jnp.float32),
            pltpu.VMEM((rows, 256, 256), jnp.bfloat16),
            pltpu.VMEM((blocks, PX, 128), jnp.bfloat16),
            pltpu.VMEM(edge, jnp.float32),
            pltpu.VMEM(edge, jnp.float32),
            pltpu.VMEM(edge, jnp.float32),
            pltpu.VMEM(edge, jnp.float32),
            pltpu.VMEM((2, blocks, 16, 128), jnp.bfloat16),
            pltpu.VMEM(flat, jnp.float32),
            pltpu.VMEM(flat, jnp.float32),
            pltpu.VMEM((2 * tiles, blocks), jnp.bfloat16),
            pltpu.VMEM((2 * tiles * 8, 128), jnp.float32),
            pltpu.VMEM((8, 128), jnp.float32),
            pltpu.VMEM((devices, 8, 128), jnp.float32),
            dma((devices,)),
            dma((devices,)),
            dma((2, devices)),
            dma((2, devices)),
            dma,
            dma((2, 2)),
            dma((2, 2)),
            dma((2, devices)),
            dma((2, devices)),
            dma((devices,)),
            dma((devices,)),
        ],
        compiler_params=pltpu.CompilerParams(
            collective_id=0, has_side_effects=True, vmem_limit_bytes=48 * 1024 * 1024
        ),
    )(slot, block, diag, ask, way, old, scale, pixels, gains, band)


def per_device(
    iterate, residual, direction, precond, patch_ids, pixel_in, weights, filter_diag, filter_band
):
    det_rows, time_blocks = patch_ids.shape
    spans = lax.axis_size("tm")
    devices = lax.axis_size("det") * spans
    blocks = det_rows * time_blocks
    per_owner = blocks // devices
    own_patches = iterate.shape[1] // PX
    patch_flat = patch_ids.reshape(blocks)
    owners = patch_flat // own_patches
    numbers = jnp.arange(blocks, dtype=jnp.int32)
    earlier = (owners[:, None] == owners[None, :]) & (numbers[None, :] < numbers[:, None])
    slot = owners * per_owner + jnp.sum(earlier.astype(jnp.int32), axis=1)
    packed = numbers * own_patches + patch_flat % own_patches
    by_slot = jnp.sum(jnp.where(numbers[:, None] == slot[None, :], packed[None, :], 0), axis=1)
    block = by_slot // own_patches
    requests = (by_slot % own_patches).reshape(devices, per_owner)
    requests = jnp.pad(requests, ((0, 0), (0, 128 - per_owner)))[:, None, :]
    image_map, factor = one_step(
        slot, block, filter_diag, requests, direction, residual, precond[None, :],
        pixel_in, weights, filter_band, spans, devices,
    )
    step_size, ratio = factor[:, 0:1], factor[:, 1:2]
    new_iterate = iterate + step_size * direction
    new_residual = residual - step_size * image_map
    new_direction = precond * new_residual + ratio * direction
    return (new_iterate, new_residual, new_direction)


def solution(mesh):
    in_specs = (
        P(None, ("det", "tm")),
        P(None, ("det", "tm")),
        P(None, ("det", "tm")),
        P(("det", "tm")),
        P("det", "tm"),
        P("det", "tm"),
        P("det", "tm"),
        P("det"),
        P("det", None),
    )
    out_specs = (P(None, ("det", "tm")), P(None, ("det", "tm")), P(None, ("det", "tm")))
    return jax.shard_map(
        per_device, mesh=mesh, in_specs=in_specs, out_specs=out_specs, check_vma=False
    )
```

```python
import functools

import jax
import jax.numpy as jnp
from jax import lax
from jax.experimental import pallas as pl
from jax.experimental.pallas import tpu as pltpu
from jax.sharding import PartitionSpec as P

PX = 64
MESH = pl.DeviceIdType.MESH


def halves(values):
    top = values.astype(jnp.bfloat16)
    return top, (values - top.astype(jnp.float32)).astype(jnp.bfloat16)


PARTS = 4


def vmem(count):
    return [pl.BlockSpec(memory_space=pltpu.VMEM)] * count


def smem(count):
    return [pl.BlockSpec(memory_space=pltpu.SMEM)] * count


def partners_of(groups, spans):
    group, span = lax.axis_index("det"), lax.axis_index("tm")
    me = group * spans + span
    shift = spans.bit_length() - 1

    def place(mask):
        return (group ^ (mask >> shift), span ^ (mask & (spans - 1)))

    return me, group, span, place


def remote(src, dst, sent, got, device):
    return pltpu.make_async_remote_copy(
        src_ref=src, dst_ref=dst, send_sem=sent, recv_sem=got, device_id=device, device_id_type=MESH
    )


def step_kernel(
    groups, spans,
    slot_ref, block_ref, diag_ref, ask_ref, way_hbm, old_hbm, scale_hbm, pixel_hbm, gain_hbm, band_ref,
    image_ref, factor_ref,
    way_ref, old_ref, scale_ref, pixel_ref, gain_ref,
    numbers, asked, table, served, patches, pixels, turned, gains, turned_gains, line, bands, hot,
    head, tail, before, after, cells, part, collected, spread, image, sums, held,
    load_sem, ask_sent, ask_got, local, sent, got, edge_sent, edge_got, back_sent, back_got,
    sum_sent, sum_got,
):
    devices = groups * spans
    me, group, span, place = partners_of(groups, spans)
    rows = pixel_ref.shape[0]
    blocks = block_ref.shape[0]
    per_row = blocks // rows
    per_owner = blocks // devices
    pairs = per_owner // 2
    half = rows // 2
    tiles = way_ref.shape[1] // 128
    deep = pairs * 8
    others = devices - 1
    width = devices // PARTS
    left = lax.broadcasted_iota(jnp.int32, (8, 128), 1) < 64

    loads = [
        pltpu.make_async_copy(src, dst, load_sem.at[i])
        for i, (src, dst) in enumerate(
            [(way_hbm, way_ref), (pixel_hbm, pixel_ref), (gain_hbm, gain_ref), (old_hbm, old_ref), (scale_hbm, scale_ref)]
        )
    ]
    for load in loads:
        load.start()

    barrier = pltpu.get_barrier_semaphore()

    def partners(run):
        @pl.loop(0, others)
        def _(n):
            run(others - n)

    @functools.partial(partners)
    def _(mask):
        pl.semaphore_signal(barrier, inc=1, device_id=place(mask), device_id_type=MESH)

    asked[0] = ask_ref[me]
    loads[0].wait()

    @pl.loop(0, tiles, unroll=2)
    def _(q):
        for h in range(2):
            tile = way_ref[8 * h : 8 * h + 8, pl.ds(pl.multiple_of(q * 128, 128), 128)]
            table[0, h, q] = tile
            table[1, h, q] = pltpu.roll(tile, 64, 1)

    pl.semaphore_wait(barrier, others)

    def ask(mask):
        return remote(ask_ref.at[me ^ mask], asked.at[mask], ask_sent, ask_got, place(mask))

    def give(h, mask):
        return remote(
            served.at[h, mask], patches.at[h, mask], sent, got.at[h, mask // width], place(mask)
        )

    def whole(ref, low, high, sent_sem, got_sem):
        these = ref.at[pl.ds(low, high - low)]
        return remote(these, these, sent_sem, got_sem, place(1))

    @functools.partial(partners)
    def _(mask):
        ask(mask).start()

    loads[1].wait()
    loads[2].wait()
    for r in range(0, rows, 8):
        for j in range(per_row):
            these = pl.ds(r * per_row + j, 8, stride=per_row)
            pixel = pixel_ref[r : r + 8, 128 * j : 128 * j + 128]
            gain = gain_ref[r : r + 8, 128 * j : 128 * j + 128]
            pixels[these, :] = pixel
            turned[these, :] = pltpu.roll(pixel, 64, 1)
            gains[these, :] = gain
            turned_gains[these, :] = pltpu.roll(gain, 64, 1)

    whole(asked, 1, devices, ask_sent, ask_got).wait_recv()
    move = pltpu.make_async_copy(asked, numbers, local)
    move.start()
    move.wait()

    def serve(h, mask, dst):
        for i in range(pairs):
            a, b = numbers[mask, 0, 2 * i], numbers[mask, 0, 2 * i + 1]
            dst[h, mask, i] = jnp.where(left, table[a & 1, h, a >> 1], table[1 - (b & 1), h, b >> 1])

    for h in range(2):

        @functools.partial(partners)
        def _(mask):
            serve(h, mask, served)
            give(h, mask).start()

        serve(h, 0, patches)


    lane = lax.broadcasted_iota(jnp.int32, (1, 128), 1)
    band = jnp.concatenate([band_ref[...], jnp.zeros((rows, 128 - band_ref.shape[1]), jnp.float32)], axis=1)
    wanted = jnp.broadcast_to(jnp.where(lane < 64, 63 - lane, jnp.maximum(lane - 65, 0)), (rows, 128))
    upper = jnp.take_along_axis(band, wanted, axis=1)
    lower = jnp.where(
        lane == 0, jnp.take_along_axis(band, jnp.full((rows, 128), 63, jnp.int32), axis=1), 0.0
    )
    held_bands = jnp.concatenate([lower, upper], axis=1)

    wide_lane = lax.broadcasted_iota(jnp.int32, (1, 256), 1)
    for d in range(rows):
        base = jnp.where(wide_lane == 192, diag_ref[d], held_bands[d : d + 1])
        around = pltpu.roll(jnp.broadcast_to(base, (128, 256)), 0, 1, stride=1, stride_axis=0)
        bands[d] = jnp.concatenate(
            [
                jnp.concatenate(halves(around[:, :128]), axis=1),
                jnp.concatenate(halves(around[:, 128:]), axis=1),
            ],
            axis=0,
        )

    spot = lax.broadcasted_iota(jnp.int32, (PX, 128), 0)

    @pl.loop(0, blocks, unroll=2)
    def _(s):
        pixel = jnp.broadcast_to(pixels[pl.ds(block_ref[s], 1), :], (PX, 128))
        hot[s] = jnp.where(spot == pixel, 1.0, 0.0).astype(jnp.bfloat16)

    asks = asked[:, 0, :]
    even = jnp.concatenate(
        [jnp.broadcast_to(asks[:, 2 * i : 2 * i + 1], (devices, 2 * tiles)) for i in range(pairs)], axis=0
    )
    odd = jnp.concatenate(
        [jnp.broadcast_to(asks[:, 2 * i + 1 : 2 * i + 2], (devices, 2 * tiles)) for i in range(pairs)], axis=0
    )
    column = lax.broadcasted_iota(jnp.int32, even.shape, 1)
    first = column < tiles
    target = jnp.where(first, 2 * column, 2 * (column - tiles) + 1)
    straight = jnp.where(jnp.where(first, even, odd) == target, 1.0, 0.0)
    crossed = jnp.where(jnp.where(first, odd, even) == target, 1.0, 0.0)
    spread[...] = jnp.concatenate([straight.T, crossed.T], axis=1).astype(jnp.bfloat16)

    def scan(h, mask):
        for i in range(pairs):
            patch = patches[h, mask, i]
            for side in range(2):
                s = (me ^ mask) * per_owner + 2 * i + side
                b = block_ref[s]
                pixel = jnp.broadcast_to(turned[pl.ds(b, 1), :], (8, 128)) + 64 * side
                gain = jnp.broadcast_to(turned_gains[pl.ds(b, 1), :], (8, 128))
                line[h, s] = jnp.take_along_axis(patch, pixel, axis=1) * gain

    def arrive(h):
        scan(h, 0)
        for g in reversed(range(PARTS)):
            low, high = max(1, g * width), (g + 1) * width
            whole(patches.at[h], low, high, sent, got.at[h, g]).wait_recv()

            @pl.loop(low, high)
            def _(mask):
                scan(h, mask)

    forth = [
        remote(tail.at[h], before.at[h], edge_sent.at[h, 0], edge_got.at[h, 0],
               (group, lax.rem(span + 1, spans)))
        for h in range(2)
    ]
    back = [
        remote(head.at[h], after.at[h], edge_sent.at[h, 1], edge_got.at[h, 1],
               (group, lax.rem(span + spans - 1, spans)))
        for h in range(2)
    ]

    def edges(h):
        @pl.loop(0, half)
        def _(d):
            start, end = d * per_row, d * per_row + per_row - 1
            far = half * per_row
            head[h, d] = jnp.where(
                left, pltpu.roll(line[h, slot_ref[start]], 64, 1), line[h, slot_ref[start + far]]
            )
            tail[h, d] = jnp.where(
                left, line[h, slot_ref[end]], pltpu.roll(line[h, slot_ref[end + far]], 64, 1)
            )

        forth[h].start()
        back[h].start()

    def edges_in(h):
        forth[h].wait()
        back[h].wait()

        @pl.when(span == 0)
        def _():
            before[h] = jnp.zeros_like(before[h])

        @pl.when(span == spans - 1)
        def _():
            after[h] = jnp.zeros_like(after[h])

    def one_row(h, d, early, late):
        mine = [early] + [line[h, slot_ref[d * per_row + j]] for j in range(per_row)] + [late]
        shifted = [jnp.where(left, mine[m], mine[m + 1]) for m in range(per_row + 1)]
        near = jnp.concatenate(shifted[:-1], axis=0)
        far = jnp.concatenate(shifted[1:], axis=0)
        wide = jnp.concatenate(
            [jnp.concatenate(halves(near), axis=0), jnp.concatenate(halves(far), axis=0)], axis=1
        )
        made = jnp.dot(wide, bands[d], preferred_element_type=jnp.float32)
        n = 8 * per_row
        filtered = made[:n, :128] + (made[n:, :128] + made[:n, 128:])
        for j in range(per_row):
            gain = jnp.broadcast_to(gains[pl.ds(d * per_row + j, 1), :], (8, 128))
            values = filtered[8 * j : 8 * j + 8] * gain
            top = values.astype(jnp.bfloat16).astype(jnp.float32)
            cells[h, d * per_row + j] = jnp.concatenate([top, values - top], axis=0).astype(jnp.bfloat16)

    def filter_all(h):
        @pl.loop(0, half)
        def _(d):
            early, late = before[h, d], after[h, d]
            one_row(h, d, early, pltpu.roll(late, 64, 1))
            one_row(h, d + half, pltpu.roll(early, 64, 1), late)

    blank = jnp.zeros((PX, 128), jnp.bfloat16)

    def project(h, mask, dst):
        for i in range(pairs):
            s = (me ^ mask) * per_owner + 2 * i
            both = jnp.concatenate([cells[h, block_ref[s]], cells[h, block_ref[s + 1]]], axis=1)
            grid = jnp.concatenate(
                [
                    jnp.concatenate([hot[s], blank], axis=1),
                    jnp.concatenate([blank, hot[s + 1]], axis=1),
                ],
                axis=0,
            )
            added = lax.dot_general(
                both, grid, (((1,), (1,)), ((), ())), preferred_element_type=jnp.float32
            )
            where = (h * devices + mask) * deep + 8 * i
            dst[pl.ds(pl.multiple_of(where, 8), 8), :] = added[:8] + added[8:]

    def rows_of(h, mask, count):
        return pl.ds(pl.multiple_of((h * devices + mask) * deep, 8), count * deep)

    def send_back(h, mask):
        these = rows_of(h, mask, 1)
        return remote(
            part.at[these], collected.at[these], back_sent, back_got.at[h, mask // width], place(mask)
        )

    def project_all(h):
        @functools.partial(partners)
        def _(mask):
            project(h, mask, part)
            send_back(h, mask).start()

        project(h, 0, collected)

    def gather_up(h):
        for g in reversed(range(PARTS)):
            low, high = max(1, g * width), (g + 1) * width
            these = collected.at[rows_of(h, low, high - low)]
            remote(these, these, back_sent, back_got.at[h, g], place(1)).wait_recv()

        wide_left = lax.broadcasted_iota(jnp.int32, (tiles, 128), 1) < 64
        for k in range(8):
            came = jnp.concatenate(
                [
                    collected[pl.ds(h * devices * deep + 8 * i + k, devices, stride=deep), :]
                    for i in range(pairs)
                ],
                axis=0,
            )
            came = jnp.concatenate([came, pltpu.roll(came, 64, 1)], axis=0)
            total = jnp.dot(
                spread[...], jnp.concatenate(halves(came), axis=1), preferred_element_type=jnp.float32
            )
            total = total[:, :128] + total[:, 128:]
            image[pl.ds(h * tiles * 8 + k, tiles, stride=8), :] = jnp.where(
                wide_left, total[:tiles], total[tiles:]
            )

        zero = jnp.zeros((8, 128), jnp.float32)

        def add(q, totals):
            these = pl.ds(pl.multiple_of(q * 128, 128), 128)
            tile = image[pl.ds(pl.multiple_of((h * tiles + q) * 8, 8), 8), :]
            image_ref[8 * h : 8 * h + 8, these] = tile
            old = old_ref[8 * h : 8 * h + 8, these]
            scale = jnp.broadcast_to(scale_ref[:, these], (8, 128))
            way = way_ref[8 * h : 8 * h + 8, these]
            lean = scale * old
            return (
                totals[0] + old * lean,
                totals[1] + way * tile,
                totals[2] + tile * lean,
                totals[3] + tile * (scale * tile),
            )

        return [
            jnp.sum(total, axis=1, keepdims=True)
            for total in lax.fori_loop(0, tiles, add, (zero,) * 4, unroll=4)
        ]

    arrive(0)
    edges(0)
    edges_in(0)
    filter_all(0)
    project_all(0)
    arrive(1)
    edges(1)
    edges_in(1)
    filter_all(1)
    project_all(1)
    whole(ask_ref, 1, devices, ask_sent, ask_got).wait_send()
    for h in range(2):
        whole(served.at[h], 1, devices, sent, sent).wait_send()
    loads[3].wait()
    loads[4].wait()

    lanes = lax.broadcasted_iota(jnp.int32, (8, 128), 1)
    places = lax.broadcasted_iota(jnp.int32, (8, 128), 0)
    row = jnp.zeros((8, 128), jnp.float32)
    for h in range(2):
        for i, total in enumerate(gather_up(h)):
            row = jnp.where(lanes == places * 8 + 4 * h + i, total, row)
    sums[...] = jnp.sum(row, axis=0, keepdims=True)

    def give_sums(mask):
        return remote(sums, held.at[mask], sum_sent, sum_got, place(mask))

    @functools.partial(partners)
    def _(mask):
        give_sums(mask).start()

    held[0] = sums[...]
    for h in range(2):
        these = part.at[rows_of(h, 1, others)]
        remote(these, these, back_sent, back_sent, place(1)).wait_send()
    whole(held, 1, devices, sum_sent, sum_got).wait()
    total = jnp.broadcast_to(jnp.sum(held[...], axis=0), (8, 128))
    for h in range(2):
        norm_old, curvature, cross, square = (
            jnp.take_along_axis(total, places * 8 + 4 * h + i, axis=1) for i in range(4)
        )
        step_size = norm_old / curvature
        norm_new = norm_old - step_size * (2.0 * cross - step_size * square)
        factor_ref[8 * h : 8 * h + 8, :] = jnp.where(lanes == 0, step_size, norm_new / norm_old)


def one_step(slot, block, diag, ask, way, old, scale, pixels, gains, band, groups, spans):
    devices = groups * spans
    blocks = slot.shape[0]
    rows = pixels.shape[0]
    pairs = blocks // devices // 2
    tiles = way.shape[1] // 128
    edge = (2, rows // 2, 8, 128)
    both = (2, devices, pairs, 8, 128)
    flat = (2 * devices * pairs * 8, 128)
    dma = pltpu.SemaphoreType.DMA
    return pl.pallas_call(
        functools.partial(step_kernel, groups, spans),
        out_shape=(
            jax.ShapeDtypeStruct(way.shape, jnp.float32),
            jax.ShapeDtypeStruct((way.shape[0], 128), jnp.float32),
        ),
        in_specs=smem(3) + vmem(1) + [pl.BlockSpec(memory_space=pltpu.HBM)] * 5 + vmem(1),
        out_specs=tuple(vmem(2)),
        scratch_shapes=[
            pltpu.VMEM(way.shape, jnp.float32),
            pltpu.VMEM(old.shape, jnp.float32),
            pltpu.VMEM(scale.shape, jnp.float32),
            pltpu.VMEM(pixels.shape, jnp.int32),
            pltpu.VMEM(gains.shape, jnp.float32),
            pltpu.SMEM(ask.shape, jnp.int32),
            pltpu.VMEM(ask.shape, jnp.int32),
            pltpu.VMEM((2, 2, tiles, 8, 128), jnp.float32),
            pltpu.VMEM(both, jnp.float32),
            pltpu.VMEM(both, jnp.float32),
            pltpu.VMEM((blocks, 128), jnp.int32),
            pltpu.VMEM((blocks, 128), jnp.int32),
            pltpu.VMEM((blocks, 128), jnp.float32),
            pltpu.VMEM((blocks, 128), jnp.float32),
            pltpu.VMEM((2, blocks, 8, 128), jnp.float32),
            pltpu.VMEM((rows, 256, 256), jnp.bfloat16),
            pltpu.VMEM((blocks, PX, 128), jnp.bfloat16),
            pltpu.VMEM(edge, jnp.float32),
            pltpu.VMEM(edge, jnp.float32),
            pltpu.VMEM(edge, jnp.float32),
            pltpu.VMEM(edge, jnp.float32),
            pltpu.VMEM((2, blocks, 16, 128), jnp.bfloat16),
            pltpu.VMEM(flat, jnp.float32),
            pltpu.VMEM(flat, jnp.float32),
            pltpu.VMEM((2 * tiles, blocks), jnp.bfloat16),
            pltpu.VMEM((2 * tiles * 8, 128), jnp.float32),
            pltpu.VMEM((1, 128), jnp.float32),
            pltpu.VMEM((devices, 1, 128), jnp.float32),
            dma((5,)),
            dma,
            dma,
            dma,
            dma,
            dma((2, PARTS)),
            dma((2, 2)),
            dma((2, 2)),
            dma,
            dma((2, PARTS)),
            dma,
            dma,
        ],
        compiler_params=pltpu.CompilerParams(
            collective_id=0, has_side_effects=True, vmem_limit_bytes=48 * 1024 * 1024
        ),
    )(slot, block, diag, ask, way, old, scale, pixels, gains, band)


def per_device(
    iterate, residual, direction, precond, patch_ids, pixel_in, weights, filter_diag, filter_band
):
    det_rows, time_blocks = patch_ids.shape
    groups, spans = lax.axis_size("det"), lax.axis_size("tm")
    devices = groups * spans
    blocks = det_rows * time_blocks
    per_owner = blocks // devices
    own_patches = iterate.shape[1] // PX
    patch_flat = patch_ids.reshape(blocks)
    owners = patch_flat // own_patches
    numbers = jnp.arange(blocks, dtype=jnp.int32)
    earlier = (owners[:, None] == owners[None, :]) & (numbers[None, :] < numbers[:, None])
    slot = owners * per_owner + jnp.sum(earlier.astype(jnp.int32), axis=1)
    packed = numbers * own_patches + patch_flat % own_patches
    by_slot = jnp.sum(jnp.where(numbers[:, None] == slot[None, :], packed[None, :], 0), axis=1)
    block = by_slot // own_patches
    requests = (by_slot % own_patches).reshape(devices, per_owner)
    requests = jnp.pad(requests, ((0, 0), (0, 128 - per_owner)))[:, None, :]
    image_map, factor = one_step(
        slot, block, filter_diag, requests, direction, residual, precond[None, :],
        pixel_in, weights, filter_band, groups, spans,
    )
    step_size, ratio = factor[:, 0:1], factor[:, 1:2]
    new_iterate = iterate + step_size * direction
    new_residual = residual - step_size * image_map
    new_direction = precond * new_residual + ratio * direction
    return (new_iterate, new_residual, new_direction)


def solution(mesh):
    in_specs = (
        P(None, ("det", "tm")),
        P(None, ("det", "tm")),
        P(None, ("det", "tm")),
        P(("det", "tm")),
        P("det", "tm"),
        P("det", "tm"),
        P("det", "tm"),
        P("det"),
        P("det", None),
    )
    out_specs = (P(None, ("det", "tm")), P(None, ("det", "tm")), P(None, ("det", "tm")))
    return jax.shard_map(
        per_device, mesh=mesh, in_specs=in_specs, out_specs=out_specs, check_vma=False
    )
```

```python
import functools

import jax
import jax.numpy as jnp
from jax import lax
from jax.experimental import pallas as pl
from jax.experimental.pallas import tpu as pltpu
from jax.sharding import PartitionSpec as P

PX = 64
MESH = pl.DeviceIdType.MESH


def halves(values):
    top = values.astype(jnp.bfloat16)
    return top, (values - top.astype(jnp.float32)).astype(jnp.bfloat16)


PARTS = 4


def vmem(count):
    return [pl.BlockSpec(memory_space=pltpu.VMEM)] * count


def smem(count):
    return [pl.BlockSpec(memory_space=pltpu.SMEM)] * count


def partners_of(groups, spans):
    group, span = lax.axis_index("det"), lax.axis_index("tm")
    me = group * spans + span
    shift = spans.bit_length() - 1

    def place(mask):
        return (group ^ (mask >> shift), span ^ (mask & (spans - 1)))

    return me, group, span, place


def remote(src, dst, sent, got, device):
    return pltpu.make_async_remote_copy(
        src_ref=src, dst_ref=dst, send_sem=sent, recv_sem=got, device_id=device, device_id_type=MESH
    )


def step_kernel(
    groups, spans,
    diag_ref, patch_ref, way_hbm, old_hbm, scale_hbm, pixel_hbm, gain_hbm, band_ref,
    image_ref, factor_ref,
    way_ref, old_ref, scale_ref, pixel_ref, gain_ref,
    slot_ref, block_ref, slots, listed, ask_ref, numbers, asked, table, served, patches, pixels, turned, gains, turned_gains, line, bands, hot,
    head, tail, before, after, cells, part, collected, spread, image, sums, held,
    load_sem, ask_sent, ask_got, local, list_sem, sent, got, edge_sent, edge_got, back_sent, back_got,
    sum_sent, sum_got,
):
    devices = groups * spans
    me, group, span, place = partners_of(groups, spans)
    rows = pixel_ref.shape[0]
    blocks = block_ref.shape[1]
    per_row = blocks // rows
    per_owner = blocks // devices
    pairs = per_owner // 2
    half = rows // 2
    tiles = way_ref.shape[1] // 128
    deep = pairs * 8
    others = devices - 1
    width = devices // PARTS
    left = lax.broadcasted_iota(jnp.int32, (8, 128), 1) < 64

    loads = [
        pltpu.make_async_copy(src, dst, load_sem.at[i])
        for i, (src, dst) in enumerate(
            [(way_hbm, way_ref), (pixel_hbm, pixel_ref), (gain_hbm, gain_ref), (old_hbm, old_ref), (scale_hbm, scale_ref)]
        )
    ]
    barrier = pltpu.get_barrier_semaphore()

    def partners(run):
        @pl.loop(0, others)
        def _(n):
            run(others - n)

    @functools.partial(partners)
    def _(mask):
        pl.semaphore_signal(barrier, inc=1, device_id=place(mask), device_id_type=MESH)

    for load in loads:
        load.start()

    lane8 = lax.broadcasted_iota(jnp.int32, (8, 128), 1)
    row8 = lax.broadcasted_iota(jnp.int32, (8, 128), 0)
    lane1 = lax.broadcasted_iota(jnp.int32, (1, 128), 1)
    square_row = lax.broadcasted_iota(jnp.int32, (128, 128), 0)
    square_lane = lax.broadcasted_iota(jnp.int32, (128, 128), 1)
    own_patches = 2 * tiles
    own_shift = own_patches.bit_length() - 1
    row_shift = rows.bit_length() - 1
    chunks = range(blocks // 128)

    def as_column(row):
        return jnp.broadcast_to(row, (128, 128)).T

    def down(values):
        return jnp.sum(values, axis=0, keepdims=True)

    padded = jnp.concatenate([patch_ref[...], jnp.zeros((per_row, 128 - rows), jnp.int32)], axis=1)
    repeated = jnp.take_along_axis(padded, lane8 & (rows - 1), axis=1)
    lies = [
        down(jnp.where(row8 == k * (128 // rows) + (lane8 >> row_shift), repeated, 0)) for k in chunks
    ]
    owners = [jnp.right_shift(lie, own_shift) for lie in lies]
    packed = [
        (((lane1 & (rows - 1)) * per_row + k * (128 // rows) + (lane1 >> row_shift)) << own_shift)
        + (lies[k] & (own_patches - 1))
        for k in chunks
    ]
    owner_columns = [as_column(owner) for owner in owners]
    packed_columns = [as_column(pack) for pack in packed]
    slot_rows = []
    for k in chunks:
        rank = jnp.zeros((128, 128), jnp.int32)
        for c in chunks:
            same = (owner_columns[c] == owners[k]) & (square_row + 128 * c < square_lane + 128 * k)
            rank = rank + jnp.where(same, 1, 0)
        slot_rows.append(owners[k] * per_owner + down(rank))
        slots[:, 128 * k : 128 * k + 128] = slot_rows[k] & (blocks - 1)
    slot_columns = [as_column(row) for row in slot_rows]
    for k in chunks:
        found = jnp.zeros((128, 128), jnp.int32)
        for c in chunks:
            found = found + jnp.where(slot_columns[c] == square_lane + 128 * k, packed_columns[c], 0)
        by_slot = down(found)
        listed[:, 128 * k : 128 * k + 128] = jnp.right_shift(by_slot, own_shift) & (blocks - 1)
        wide = jnp.broadcast_to(by_slot & (own_patches - 1), (8, 128))
        for p in range(128 // per_owner):
            turn = (128 - p * per_owner) % 128
            ask_ref[k * (128 // per_owner) + p] = (pltpu.roll(wide, turn, 1) if turn else wide)[:1]
    lists = [
        pltpu.make_async_copy(slots, slot_ref, list_sem.at[0]),
        pltpu.make_async_copy(listed, block_ref, list_sem.at[1]),
    ]
    for copy in lists:
        copy.start()
    asked[0] = ask_ref[me]
    loads[0].wait()

    @pl.loop(0, tiles, unroll=2)
    def _(q):
        for h in range(2):
            tile = way_ref[8 * h : 8 * h + 8, pl.ds(pl.multiple_of(q * 128, 128), 128)]
            table[0, h, q] = tile
            table[1, h, q] = pltpu.roll(tile, 64, 1)

    pl.semaphore_wait(barrier, others)

    def ask(mask):
        return remote(ask_ref.at[me ^ mask], asked.at[mask], ask_sent, ask_got, place(mask))

    def give(h, mask):
        return remote(
            served.at[h, mask], patches.at[h, mask], sent, got.at[h, mask // width], place(mask)
        )

    def whole(ref, low, high, sent_sem, got_sem):
        these = ref.at[pl.ds(low, high - low)]
        return remote(these, these, sent_sem, got_sem, place(1))

    @functools.partial(partners)
    def _(mask):
        ask(mask).start()

    whole(asked, 1, devices, ask_sent, ask_got).wait_recv()
    move = pltpu.make_async_copy(asked, numbers, local)
    move.start()
    move.wait()

    def serve(h, mask, dst):
        for i in range(pairs):
            a, b = numbers[mask, 0, 2 * i], numbers[mask, 0, 2 * i + 1]
            dst[h, mask, i] = jnp.where(left, table[a & 1, h, a >> 1], table[1 - (b & 1), h, b >> 1])

    def part_of(g):
        return max(1, g * width), (g + 1) * width

    def offer(h, g):
        low, high = part_of(g)

        @pl.loop(low, high)
        def _(mask):
            serve(h, mask, served)
            give(h, mask).start()

    for g in reversed(range(PARTS)):
        offer(0, g)
    for h in range(2):
        serve(h, 0, patches)

    loads[1].wait()
    loads[2].wait()
    for r in range(0, rows, 8):
        for j in range(per_row):
            these = pl.ds(r * per_row + j, 8, stride=per_row)
            pixel = pixel_ref[r : r + 8, 128 * j : 128 * j + 128]
            gain = gain_ref[r : r + 8, 128 * j : 128 * j + 128]
            pixels[these, :] = pixel
            turned[these, :] = pltpu.roll(pixel, 64, 1)
            gains[these, :] = gain
            turned_gains[these, :] = pltpu.roll(gain, 64, 1)

    for copy in lists:
        copy.wait()

    lane = lax.broadcasted_iota(jnp.int32, (1, 128), 1)
    band = jnp.concatenate([band_ref[...], jnp.zeros((rows, 128 - band_ref.shape[1]), jnp.float32)], axis=1)
    wanted = jnp.broadcast_to(jnp.where(lane < 64, 63 - lane, jnp.maximum(lane - 65, 0)), (rows, 128))
    upper = jnp.take_along_axis(band, wanted, axis=1)
    lower = jnp.where(
        lane == 0, jnp.take_along_axis(band, jnp.full((rows, 128), 63, jnp.int32), axis=1), 0.0
    )
    held_bands = jnp.concatenate([lower, upper], axis=1)

    wide_lane = lax.broadcasted_iota(jnp.int32, (1, 256), 1)
    for d in range(rows):
        base = jnp.where(wide_lane == 192, diag_ref[d], held_bands[d : d + 1])
        around = pltpu.roll(jnp.broadcast_to(base, (128, 256)), 0, 1, stride=1, stride_axis=0)
        bands[d] = jnp.concatenate(
            [
                jnp.concatenate(halves(around[:, :128]), axis=1),
                jnp.concatenate(halves(around[:, 128:]), axis=1),
            ],
            axis=0,
        )

    spot = lax.broadcasted_iota(jnp.int32, (PX, 128), 0)

    @pl.loop(0, blocks, unroll=2)
    def _(s):
        pixel = jnp.broadcast_to(pixels[pl.ds(block_ref[0, s], 1), :], (PX, 128))
        hot[s] = jnp.where(spot == pixel, 1.0, 0.0).astype(jnp.bfloat16)

    asks = asked[:, 0, :]
    even = jnp.concatenate(
        [jnp.broadcast_to(asks[:, 2 * i : 2 * i + 1], (devices, 2 * tiles)) for i in range(pairs)], axis=0
    )
    odd = jnp.concatenate(
        [jnp.broadcast_to(asks[:, 2 * i + 1 : 2 * i + 2], (devices, 2 * tiles)) for i in range(pairs)], axis=0
    )
    column = lax.broadcasted_iota(jnp.int32, even.shape, 1)
    first = column < tiles
    target = jnp.where(first, 2 * column, 2 * (column - tiles) + 1)
    straight = jnp.where(jnp.where(first, even, odd) == target, 1.0, 0.0)
    crossed = jnp.where(jnp.where(first, odd, even) == target, 1.0, 0.0)
    spread[...] = jnp.concatenate([straight.T, crossed.T], axis=1).astype(jnp.bfloat16)

    def scan(h, mask):
        for i in range(pairs):
            patch = patches[h, mask, i]
            for side in range(2):
                s = (me ^ mask) * per_owner + 2 * i + side
                b = block_ref[0, s]
                pixel = jnp.broadcast_to(turned[pl.ds(b, 1), :], (8, 128)) + 64 * side
                gain = jnp.broadcast_to(turned_gains[pl.ds(b, 1), :], (8, 128))
                line[h, s] = jnp.take_along_axis(patch, pixel, axis=1) * gain

    def arrive(h):
        scan(h, 0)
        for g in reversed(range(PARTS)):
            low, high = part_of(g)
            whole(patches.at[h], low, high, sent, got.at[h, g]).wait_recv()
            if h == 0 and g == PARTS // 2:
                for later in reversed(range(g, PARTS)):
                    offer(1, later)

            @pl.loop(low, high)
            def _(mask):
                scan(h, mask)

        if h == 0:
            for later in reversed(range(PARTS // 2)):
                offer(1, later)

    forth = [
        remote(tail.at[h], before.at[h], edge_sent.at[h, 0], edge_got.at[h, 0],
               (group, lax.rem(span + 1, spans)))
        for h in range(2)
    ]
    back = [
        remote(head.at[h], after.at[h], edge_sent.at[h, 1], edge_got.at[h, 1],
               (group, lax.rem(span + spans - 1, spans)))
        for h in range(2)
    ]

    def edges(h):
        @pl.loop(0, half)
        def _(d):
            start, end = d, d + (per_row - 1) * rows
            head[h, d] = jnp.where(
                left, pltpu.roll(line[h, slot_ref[0, start]], 64, 1), line[h, slot_ref[0, start + half]]
            )
            tail[h, d] = jnp.where(
                left, line[h, slot_ref[0, end]], pltpu.roll(line[h, slot_ref[0, end + half]], 64, 1)
            )

        forth[h].start()
        back[h].start()

    def edges_in(h):
        forth[h].wait()
        back[h].wait()

        @pl.when(span == 0)
        def _():
            before[h] = jnp.zeros_like(before[h])

        @pl.when(span == spans - 1)
        def _():
            after[h] = jnp.zeros_like(after[h])

    def one_row(h, d, early, late):
        mine = [early] + [line[h, slot_ref[0, j * rows + d]] for j in range(per_row)] + [late]
        shifted = [jnp.where(left, mine[m], mine[m + 1]) for m in range(per_row + 1)]
        near = jnp.concatenate(shifted[:-1], axis=0)
        far = jnp.concatenate(shifted[1:], axis=0)
        wide = jnp.concatenate(
            [jnp.concatenate(halves(near), axis=0), jnp.concatenate(halves(far), axis=0)], axis=1
        )
        made = jnp.dot(wide, bands[d], preferred_element_type=jnp.float32)
        n = 8 * per_row
        filtered = made[:n, :128] + (made[n:, :128] + made[:n, 128:])
        for j in range(per_row):
            gain = jnp.broadcast_to(gains[pl.ds(d * per_row + j, 1), :], (8, 128))
            values = filtered[8 * j : 8 * j + 8] * gain
            top = values.astype(jnp.bfloat16).astype(jnp.float32)
            cells[h, d * per_row + j] = jnp.concatenate([top, values - top], axis=0).astype(jnp.bfloat16)

    def filter_all(h):
        @pl.loop(0, half)
        def _(d):
            early, late = before[h, d], after[h, d]
            one_row(h, d, early, pltpu.roll(late, 64, 1))
            one_row(h, d + half, pltpu.roll(early, 64, 1), late)

    blank = jnp.zeros((PX, 128), jnp.bfloat16)

    def project(h, mask, dst):
        for i in range(pairs):
            s = (me ^ mask) * per_owner + 2 * i
            both = jnp.concatenate([cells[h, block_ref[0, s]], cells[h, block_ref[0, s + 1]]], axis=1)
            grid = jnp.concatenate(
                [
                    jnp.concatenate([hot[s], blank], axis=1),
                    jnp.concatenate([blank, hot[s + 1]], axis=1),
                ],
                axis=0,
            )
            added = lax.dot_general(
                both, grid, (((1,), (1,)), ((), ())), preferred_element_type=jnp.float32
            )
            where = (h * devices + mask) * deep + 8 * i
            dst[pl.ds(pl.multiple_of(where, 8), 8), :] = added[:8] + added[8:]

    def rows_of(h, mask, count):
        return pl.ds(pl.multiple_of((h * devices + mask) * deep, 8), count * deep)

    def send_back(h, mask):
        these = rows_of(h, mask, 1)
        return remote(
            part.at[these], collected.at[these], back_sent, back_got.at[h, mask // width], place(mask)
        )

    def project_part(h, g):
        low, high = part_of(g)

        @pl.loop(low, high)
        def _(mask):
            project(h, mask, part)
            send_back(h, mask).start()

        if g == 0:
            project(h, 0, collected)

    def gather_up(h):
        for g in reversed(range(PARTS)):
            low, high = part_of(g)
            these = collected.at[rows_of(h, low, high - low)]
            remote(these, these, back_sent, back_got.at[h, g], place(1)).wait_recv()

        wide_left = lax.broadcasted_iota(jnp.int32, (tiles, 128), 1) < 64
        for k in range(8):
            came = jnp.concatenate(
                [
                    collected[pl.ds(h * devices * deep + 8 * i + k, devices, stride=deep), :]
                    for i in range(pairs)
                ],
                axis=0,
            )
            came = jnp.concatenate([came, pltpu.roll(came, 64, 1)], axis=0)
            total = jnp.dot(
                spread[...], jnp.concatenate(halves(came), axis=1), preferred_element_type=jnp.float32
            )
            total = total[:, :128] + total[:, 128:]
            image[pl.ds(h * tiles * 8 + k, tiles, stride=8), :] = jnp.where(
                wide_left, total[:tiles], total[tiles:]
            )

        zero = jnp.zeros((8, 128), jnp.float32)

        def add(q, totals):
            these = pl.ds(pl.multiple_of(q * 128, 128), 128)
            tile = image[pl.ds(pl.multiple_of((h * tiles + q) * 8, 8), 8), :]
            image_ref[8 * h : 8 * h + 8, these] = tile
            old = old_ref[8 * h : 8 * h + 8, these]
            scale = jnp.broadcast_to(scale_ref[:, these], (8, 128))
            way = way_ref[8 * h : 8 * h + 8, these]
            lean = scale * old
            return (
                totals[0] + old * lean,
                totals[1] + way * tile,
                totals[2] + tile * lean,
                totals[3] + tile * (scale * tile),
            )

        return [
            jnp.sum(total, axis=1, keepdims=True)
            for total in lax.fori_loop(0, tiles, add, (zero,) * 4, unroll=4)
        ]

    arrive(0)
    edges(0)
    edges_in(0)
    filter_all(0)
    for g in reversed(range(PARTS // 2, PARTS)):
        project_part(0, g)
    arrive(1)
    edges(1)
    for g in reversed(range(PARTS // 2)):
        project_part(0, g)
    edges_in(1)
    filter_all(1)
    for g in reversed(range(PARTS)):
        project_part(1, g)
    whole(ask_ref, 1, devices, ask_sent, ask_got).wait_send()
    for h in range(2):
        whole(served.at[h], 1, devices, sent, sent).wait_send()
    loads[3].wait()
    loads[4].wait()

    lanes = lax.broadcasted_iota(jnp.int32, (8, 128), 1)
    places = lax.broadcasted_iota(jnp.int32, (8, 128), 0)
    row = jnp.zeros((8, 128), jnp.float32)
    for h in range(2):
        for i, total in enumerate(gather_up(h)):
            row = jnp.where(lanes == places * 8 + 4 * h + i, total, row)
    sums[...] = jnp.sum(row, axis=0, keepdims=True)

    def give_sums(mask):
        return remote(sums, held.at[mask], sum_sent, sum_got, place(mask))

    @functools.partial(partners)
    def _(mask):
        give_sums(mask).start()

    held[0] = sums[...]
    for h in range(2):
        these = part.at[rows_of(h, 1, others)]
        remote(these, these, back_sent, back_sent, place(1)).wait_send()
    whole(held, 1, devices, sum_sent, sum_got).wait()
    total = jnp.broadcast_to(jnp.sum(held[...], axis=0), (8, 128))
    for h in range(2):
        norm_old, curvature, cross, square = (
            jnp.take_along_axis(total, places * 8 + 4 * h + i, axis=1) for i in range(4)
        )
        step_size = norm_old / curvature
        norm_new = norm_old - step_size * (2.0 * cross - step_size * square)
        factor_ref[8 * h : 8 * h + 8, :] = jnp.where(lanes == 0, step_size, norm_new / norm_old)


def one_step(diag, patch, way, old, scale, pixels, gains, band, groups, spans):
    devices = groups * spans
    rows = pixels.shape[0]
    blocks = patch.size
    pairs = blocks // devices // 2
    tiles = way.shape[1] // 128
    edge = (2, rows // 2, 8, 128)
    both = (2, devices, pairs, 8, 128)
    flat = (2 * devices * pairs * 8, 128)
    asks = (devices, 1, 128)
    dma = pltpu.SemaphoreType.DMA
    return pl.pallas_call(
        functools.partial(step_kernel, groups, spans),
        out_shape=(
            jax.ShapeDtypeStruct(way.shape, jnp.float32),
            jax.ShapeDtypeStruct((way.shape[0], 128), jnp.float32),
        ),
        in_specs=smem(1) + vmem(1) + [pl.BlockSpec(memory_space=pltpu.HBM)] * 5 + vmem(1),
        out_specs=tuple(vmem(2)),
        scratch_shapes=[
            pltpu.VMEM(way.shape, jnp.float32),
            pltpu.VMEM(old.shape, jnp.float32),
            pltpu.VMEM(scale.shape, jnp.float32),
            pltpu.VMEM(pixels.shape, jnp.int32),
            pltpu.VMEM(gains.shape, jnp.float32),
            pltpu.SMEM((1, blocks), jnp.int32),
            pltpu.SMEM((1, blocks), jnp.int32),
            pltpu.VMEM((1, blocks), jnp.int32),
            pltpu.VMEM((1, blocks), jnp.int32),
            pltpu.VMEM(asks, jnp.int32),
            pltpu.SMEM(asks, jnp.int32),
            pltpu.VMEM(asks, jnp.int32),
            pltpu.VMEM((2, 2, tiles, 8, 128), jnp.float32),
            pltpu.VMEM(both, jnp.float32),
            pltpu.VMEM(both, jnp.float32),
            pltpu.VMEM((blocks, 128), jnp.int32),
            pltpu.VMEM((blocks, 128), jnp.int32),
            pltpu.VMEM((blocks, 128), jnp.float32),
            pltpu.VMEM((blocks, 128), jnp.float32),
            pltpu.VMEM((2, blocks, 8, 128), jnp.float32),
            pltpu.VMEM((rows, 256, 256), jnp.bfloat16),
            pltpu.VMEM((blocks, PX, 128), jnp.bfloat16),
            pltpu.VMEM(edge, jnp.float32),
            pltpu.VMEM(edge, jnp.float32),
            pltpu.VMEM(edge, jnp.float32),
            pltpu.VMEM(edge, jnp.float32),
            pltpu.VMEM((2, blocks, 16, 128), jnp.bfloat16),
            pltpu.VMEM(flat, jnp.float32),
            pltpu.VMEM(flat, jnp.float32),
            pltpu.VMEM((2 * tiles, blocks), jnp.bfloat16),
            pltpu.VMEM((2 * tiles * 8, 128), jnp.float32),
            pltpu.VMEM((1, 128), jnp.float32),
            pltpu.VMEM((devices, 1, 128), jnp.float32),
            dma((5,)),
            dma,
            dma,
            dma,
            dma((2,)),
            dma,
            dma((2, PARTS)),
            dma((2, 2)),
            dma((2, 2)),
            dma,
            dma((2, PARTS)),
            dma,
            dma,
        ],
        compiler_params=pltpu.CompilerParams(
            collective_id=0, has_side_effects=True, vmem_limit_bytes=62 * 1024 * 1024
        ),
    )(diag, patch, way, old, scale, pixels, gains, band)


def per_device(
    iterate, residual, direction, precond, patch_ids, pixel_in, weights, filter_diag, filter_band
):
    groups, spans = lax.axis_size("det"), lax.axis_size("tm")
    image_map, factor = one_step(
        filter_diag, patch_ids.T, direction, residual, precond[None, :],
        pixel_in, weights, filter_band, groups, spans,
    )
    step_size, ratio = factor[:, 0:1], factor[:, 1:2]
    new_iterate = iterate + step_size * direction
    new_residual = residual - step_size * image_map
    new_direction = precond * new_residual + ratio * direction
    return (new_iterate, new_residual, new_direction)


def solution(mesh):
    in_specs = (
        P(None, ("det", "tm")),
        P(None, ("det", "tm")),
        P(None, ("det", "tm")),
        P(("det", "tm")),
        P("det", "tm"),
        P("det", "tm"),
        P("det", "tm"),
        P("det"),
        P("det", None),
    )
    out_specs = (P(None, ("det", "tm")), P(None, ("det", "tm")), P(None, ("det", "tm")))
    return jax.shard_map(
        per_device, mesh=mesh, in_specs=in_specs, out_specs=out_specs, check_vma=False
    )
```

```python
import functools

import jax
import jax.numpy as jnp
from jax import lax
from jax.experimental import pallas as pl
from jax.experimental.pallas import tpu as pltpu
from jax.sharding import PartitionSpec as P

PX = 64
MESH = pl.DeviceIdType.MESH


def halves(values):
    top = values.astype(jnp.bfloat16)
    return top, (values - top.astype(jnp.float32)).astype(jnp.bfloat16)


PARTS = 4


def vmem(count):
    return [pl.BlockSpec(memory_space=pltpu.VMEM)] * count


def smem(count):
    return [pl.BlockSpec(memory_space=pltpu.SMEM)] * count


def partners_of(groups, spans):
    group, span = lax.axis_index("det"), lax.axis_index("tm")
    me = group * spans + span
    shift = spans.bit_length() - 1

    def place(mask):
        return (group ^ (mask >> shift), span ^ (mask & (spans - 1)))

    return me, group, span, place


def remote(src, dst, sent, got, device):
    return pltpu.make_async_remote_copy(
        src_ref=src, dst_ref=dst, send_sem=sent, recv_sem=got, device_id=device, device_id_type=MESH
    )


def step_kernel(
    groups, spans,
    diag_ref, patch_ref, way_hbm, old_hbm, scale_hbm, pixel_hbm, gain_hbm, band_ref,
    image_ref, factor_ref,
    way_ref, old_ref, scale_ref, pixel_ref, gain_ref,
    slot_ref, block_ref, slots, listed, ask_ref, numbers, asked, table, served, patches, pixels, turned, gains, turned_gains, line, bands, hot,
    head, tail, before, after, cells, part, collected, spread, image, sums, held,
    load_sem, ask_sent, ask_got, local, list_sem, sent, got, edge_sent, edge_got, back_sent, back_got,
    sum_sent, sum_got,
):
    devices = groups * spans
    me, group, span, place = partners_of(groups, spans)
    rows = pixel_ref.shape[0]
    blocks = block_ref.shape[1]
    per_row = blocks // rows
    per_owner = blocks // devices
    pairs = per_owner // 2
    half = rows // 2
    tiles = way_ref.shape[1] // 128
    deep = pairs * 8
    others = devices - 1
    width = devices // PARTS
    left = lax.broadcasted_iota(jnp.int32, (8, 128), 1) < 64

    loads = [
        pltpu.make_async_copy(src, dst, load_sem.at[i])
        for i, (src, dst) in enumerate(
            [(way_hbm, way_ref), (pixel_hbm, pixel_ref), (gain_hbm, gain_ref), (old_hbm, old_ref), (scale_hbm, scale_ref)]
        )
    ]
    barrier = pltpu.get_barrier_semaphore()

    def partners(run):
        @pl.loop(0, others)
        def _(n):
            run(others - n)

    @functools.partial(partners)
    def _(mask):
        pl.semaphore_signal(barrier, inc=1, device_id=place(mask), device_id_type=MESH)

    for load in loads:
        load.start()

    lane8 = lax.broadcasted_iota(jnp.int32, (8, 128), 1)
    row8 = lax.broadcasted_iota(jnp.int32, (8, 128), 0)
    lane1 = lax.broadcasted_iota(jnp.int32, (1, 128), 1)
    square_row = lax.broadcasted_iota(jnp.int32, (128, 128), 0)
    square_lane = lax.broadcasted_iota(jnp.int32, (128, 128), 1)
    own_patches = 2 * tiles
    own_shift = own_patches.bit_length() - 1
    row_shift = rows.bit_length() - 1
    chunks = range(blocks // 128)

    def as_column(row):
        return jnp.broadcast_to(row, (128, 128)).T

    def down(values):
        return jnp.sum(values, axis=0, keepdims=True)

    padded = jnp.concatenate([patch_ref[...], jnp.zeros((per_row, 128 - rows), jnp.int32)], axis=1)
    repeated = jnp.take_along_axis(padded, lane8 & (rows - 1), axis=1)
    lies = [
        down(jnp.where(row8 == k * (128 // rows) + (lane8 >> row_shift), repeated, 0)) for k in chunks
    ]
    owners = [jnp.right_shift(lie, own_shift) for lie in lies]
    packed = [
        (((lane1 & (rows - 1)) * per_row + k * (128 // rows) + (lane1 >> row_shift)) << own_shift)
        + (lies[k] & (own_patches - 1))
        for k in chunks
    ]
    owner_columns = [as_column(owner) for owner in owners]
    packed_columns = [as_column(pack) for pack in packed]
    slot_rows = []
    for k in chunks:
        rank = jnp.zeros((128, 128), jnp.int32)
        for c in chunks:
            same = (owner_columns[c] == owners[k]) & (square_row + 128 * c < square_lane + 128 * k)
            rank = rank + jnp.where(same, 1, 0)
        slot_rows.append(owners[k] * per_owner + down(rank))
        slots[:, 128 * k : 128 * k + 128] = slot_rows[k] & (blocks - 1)
    slot_columns = [as_column(row) for row in slot_rows]
    for k in chunks:
        found = jnp.zeros((128, 128), jnp.int32)
        for c in chunks:
            found = found + jnp.where(slot_columns[c] == square_lane + 128 * k, packed_columns[c], 0)
        by_slot = down(found)
        listed[:, 128 * k : 128 * k + 128] = jnp.right_shift(by_slot, own_shift) & (blocks - 1)
        wide = jnp.broadcast_to(by_slot & (own_patches - 1), (8, 128))
        for p in range(128 // per_owner):
            turn = (128 - p * per_owner) % 128
            ask_ref[k * (128 // per_owner) + p] = (pltpu.roll(wide, turn, 1) if turn else wide)[:1]
    lists = [
        pltpu.make_async_copy(slots, slot_ref, list_sem.at[0]),
        pltpu.make_async_copy(listed, block_ref, list_sem.at[1]),
    ]
    for copy in lists:
        copy.start()
    asked[0] = ask_ref[me]
    pl.semaphore_wait(barrier, others)

    def ask(mask):
        return remote(ask_ref.at[me ^ mask], asked.at[mask], ask_sent, ask_got, place(mask))

    def give(h, mask):
        return remote(
            served.at[h, mask], patches.at[h, mask], sent, got.at[h, mask // width], place(mask)
        )

    def whole(ref, low, high, sent_sem, got_sem):
        these = ref.at[pl.ds(low, high - low)]
        return remote(these, these, sent_sem, got_sem, place(1))

    @functools.partial(partners)
    def _(mask):
        ask(mask).start()

    loads[0].wait()

    @pl.loop(0, tiles, unroll=2)
    def _(q):
        for h in range(2):
            tile = way_ref[8 * h : 8 * h + 8, pl.ds(pl.multiple_of(q * 128, 128), 128)]
            table[0, h, q] = tile
            table[1, h, q] = pltpu.roll(tile, 64, 1)

    whole(asked, 1, devices, ask_sent, ask_got).wait_recv()
    move = pltpu.make_async_copy(asked, numbers, local)
    move.start()
    move.wait()

    def serve(h, mask, dst):
        for i in range(pairs):
            a, b = numbers[mask, 0, 2 * i], numbers[mask, 0, 2 * i + 1]
            dst[h, mask, i] = jnp.where(left, table[a & 1, h, a >> 1], table[1 - (b & 1), h, b >> 1])

    def part_of(g):
        return max(1, g * width), (g + 1) * width

    def offer(h, g):
        low, high = part_of(g)

        @pl.loop(low, high)
        def _(mask):
            serve(h, mask, served)
            give(h, mask).start()

    for g in reversed(range(PARTS)):
        offer(0, g)
    for h in range(2):
        serve(h, 0, patches)

    loads[1].wait()
    loads[2].wait()
    for r in range(0, rows, 8):
        for j in range(per_row):
            these = pl.ds(r * per_row + j, 8, stride=per_row)
            pixel = pixel_ref[r : r + 8, 128 * j : 128 * j + 128]
            gain = gain_ref[r : r + 8, 128 * j : 128 * j + 128]
            pixels[these, :] = pixel
            turned[these, :] = pltpu.roll(pixel, 64, 1)
            gains[these, :] = gain
            turned_gains[these, :] = pltpu.roll(gain, 64, 1)

    for copy in lists:
        copy.wait()

    lane = lax.broadcasted_iota(jnp.int32, (1, 128), 1)
    band = jnp.concatenate([band_ref[...], jnp.zeros((rows, 128 - band_ref.shape[1]), jnp.float32)], axis=1)
    wanted = jnp.broadcast_to(jnp.where(lane < 64, 63 - lane, jnp.maximum(lane - 65, 0)), (rows, 128))
    upper = jnp.take_along_axis(band, wanted, axis=1)
    lower = jnp.where(
        lane == 0, jnp.take_along_axis(band, jnp.full((rows, 128), 63, jnp.int32), axis=1), 0.0
    )
    held_bands = jnp.concatenate([lower, upper], axis=1)

    wide_lane = lax.broadcasted_iota(jnp.int32, (1, 256), 1)
    for d in range(rows):
        base = jnp.where(wide_lane == 192, diag_ref[d], held_bands[d : d + 1])
        around = pltpu.roll(jnp.broadcast_to(base, (128, 256)), 0, 1, stride=1, stride_axis=0)
        bands[d] = jnp.concatenate(
            [
                jnp.concatenate(halves(around[:, :128]), axis=1),
                jnp.concatenate(halves(around[:, 128:]), axis=1),
            ],
            axis=0,
        )

    spot = lax.broadcasted_iota(jnp.int32, (PX, 128), 0)

    @pl.loop(0, blocks, unroll=2)
    def _(s):
        pixel = jnp.broadcast_to(pixels[pl.ds(block_ref[0, s], 1), :], (PX, 128))
        hot[s] = jnp.where(spot == pixel, 1.0, 0.0).astype(jnp.bfloat16)

    asks = asked[:, 0, :]
    even = jnp.concatenate(
        [jnp.broadcast_to(asks[:, 2 * i : 2 * i + 1], (devices, 2 * tiles)) for i in range(pairs)], axis=0
    )
    odd = jnp.concatenate(
        [jnp.broadcast_to(asks[:, 2 * i + 1 : 2 * i + 2], (devices, 2 * tiles)) for i in range(pairs)], axis=0
    )
    column = lax.broadcasted_iota(jnp.int32, even.shape, 1)
    first = column < tiles
    target = jnp.where(first, 2 * column, 2 * (column - tiles) + 1)
    straight = jnp.where(jnp.where(first, even, odd) == target, 1.0, 0.0)
    crossed = jnp.where(jnp.where(first, odd, even) == target, 1.0, 0.0)
    spread[...] = jnp.concatenate([straight.T, crossed.T], axis=1).astype(jnp.bfloat16)

    def scan(h, mask):
        for i in range(pairs):
            patch = patches[h, mask, i]
            for side in range(2):
                s = (me ^ mask) * per_owner + 2 * i + side
                b = block_ref[0, s]
                pixel = jnp.broadcast_to(turned[pl.ds(b, 1), :], (8, 128)) + 64 * side
                gain = jnp.broadcast_to(turned_gains[pl.ds(b, 1), :], (8, 128))
                line[h, s] = jnp.take_along_axis(patch, pixel, axis=1) * gain

    def arrive(h):
        scan(h, 0)
        for g in reversed(range(PARTS)):
            low, high = part_of(g)
            whole(patches.at[h], low, high, sent, got.at[h, g]).wait_recv()
            if h == 0 and g == PARTS // 2:
                for later in reversed(range(g, PARTS)):
                    offer(1, later)

            @pl.loop(low, high, unroll=2)
            def _(mask):
                scan(h, mask)


    forth = [
        remote(tail.at[h], before.at[h], edge_sent.at[h, 0], edge_got.at[h, 0],
               (group, lax.rem(span + 1, spans)))
        for h in range(2)
    ]
    back = [
        remote(head.at[h], after.at[h], edge_sent.at[h, 1], edge_got.at[h, 1],
               (group, lax.rem(span + spans - 1, spans)))
        for h in range(2)
    ]

    def edges(h):
        @pl.loop(0, half)
        def _(d):
            start, end = d, d + (per_row - 1) * rows
            head[h, d] = jnp.where(
                left, pltpu.roll(line[h, slot_ref[0, start]], 64, 1), line[h, slot_ref[0, start + half]]
            )
            tail[h, d] = jnp.where(
                left, line[h, slot_ref[0, end]], pltpu.roll(line[h, slot_ref[0, end + half]], 64, 1)
            )

        forth[h].start()
        back[h].start()

    def edges_in(h):
        forth[h].wait()
        back[h].wait()

        @pl.when(span == 0)
        def _():
            before[h] = jnp.zeros_like(before[h])

        @pl.when(span == spans - 1)
        def _():
            after[h] = jnp.zeros_like(after[h])

    def one_row(h, d, early, late):
        mine = [early] + [line[h, slot_ref[0, j * rows + d]] for j in range(per_row)] + [late]
        shifted = [jnp.where(left, mine[m], mine[m + 1]) for m in range(per_row + 1)]
        near = jnp.concatenate(shifted[:-1], axis=0)
        far = jnp.concatenate(shifted[1:], axis=0)
        wide = jnp.concatenate(
            [jnp.concatenate(halves(near), axis=0), jnp.concatenate(halves(far), axis=0)], axis=1
        )
        made = jnp.dot(wide, bands[d], preferred_element_type=jnp.float32)
        n = 8 * per_row
        filtered = made[:n, :128] + (made[n:, :128] + made[:n, 128:])
        for j in range(per_row):
            gain = jnp.broadcast_to(gains[pl.ds(d * per_row + j, 1), :], (8, 128))
            values = filtered[8 * j : 8 * j + 8] * gain
            top = values.astype(jnp.bfloat16).astype(jnp.float32)
            cells[h, d * per_row + j] = jnp.concatenate([top, values - top], axis=0).astype(jnp.bfloat16)

    def filter_all(h):
        @pl.loop(0, half, unroll=2)
        def _(d):
            early, late = before[h, d], after[h, d]
            one_row(h, d, early, pltpu.roll(late, 64, 1))
            one_row(h, d + half, pltpu.roll(early, 64, 1), late)

    blank = jnp.zeros((PX, 128), jnp.bfloat16)

    def project(h, mask, dst):
        for i in range(pairs):
            s = (me ^ mask) * per_owner + 2 * i
            both = jnp.concatenate([cells[h, block_ref[0, s]], cells[h, block_ref[0, s + 1]]], axis=1)
            grid = jnp.concatenate(
                [
                    jnp.concatenate([hot[s], blank], axis=1),
                    jnp.concatenate([blank, hot[s + 1]], axis=1),
                ],
                axis=0,
            )
            added = lax.dot_general(
                both, grid, (((1,), (1,)), ((), ())), preferred_element_type=jnp.float32
            )
            where = (h * devices + mask) * deep + 8 * i
            dst[pl.ds(pl.multiple_of(where, 8), 8), :] = added[:8] + added[8:]

    def rows_of(h, mask, count):
        return pl.ds(pl.multiple_of((h * devices + mask) * deep, 8), count * deep)

    def send_back(h, mask):
        these = rows_of(h, mask, 1)
        return remote(
            part.at[these], collected.at[these], back_sent, back_got.at[h, mask // width], place(mask)
        )

    def project_part(h, g):
        low, high = part_of(g)

        @pl.loop(low, high, unroll=min(8, high - low))
        def _(mask):
            project(h, mask, part)

        @pl.loop(low, high)
        def _(mask):
            send_back(h, mask).start()

        if g == 0:
            project(h, 0, collected)

    def gather_up(h):
        for g in reversed(range(PARTS)):
            low, high = part_of(g)
            these = collected.at[rows_of(h, low, high - low)]
            remote(these, these, back_sent, back_got.at[h, g], place(1)).wait_recv()

        wide_left = lax.broadcasted_iota(jnp.int32, (tiles, 128), 1) < 64
        for k in range(8):
            came = jnp.concatenate(
                [
                    collected[pl.ds(h * devices * deep + 8 * i + k, devices, stride=deep), :]
                    for i in range(pairs)
                ],
                axis=0,
            )
            came = jnp.concatenate([came, pltpu.roll(came, 64, 1)], axis=0)
            total = jnp.dot(
                spread[...], jnp.concatenate(halves(came), axis=1), preferred_element_type=jnp.float32
            )
            total = total[:, :128] + total[:, 128:]
            image[pl.ds(h * tiles * 8 + k, tiles, stride=8), :] = jnp.where(
                wide_left, total[:tiles], total[tiles:]
            )

        zero = jnp.zeros((8, 128), jnp.float32)

        def add(q, totals):
            these = pl.ds(pl.multiple_of(q * 128, 128), 128)
            tile = image[pl.ds(pl.multiple_of((h * tiles + q) * 8, 8), 8), :]
            image_ref[8 * h : 8 * h + 8, these] = tile
            old = old_ref[8 * h : 8 * h + 8, these]
            scale = jnp.broadcast_to(scale_ref[:, these], (8, 128))
            way = way_ref[8 * h : 8 * h + 8, these]
            lean = scale * old
            return (
                totals[0] + old * lean,
                totals[1] + way * tile,
                totals[2] + tile * lean,
                totals[3] + tile * (scale * tile),
            )

        return [
            jnp.sum(total, axis=1, keepdims=True)
            for total in lax.fori_loop(0, tiles, add, (zero,) * 4, unroll=4)
        ]

    arrive(0)
    edges(0)
    for g in reversed(range(PARTS // 2)):
        offer(1, g)
    edges_in(0)
    filter_all(0)
    for g in reversed(range(PARTS // 2, PARTS)):
        project_part(0, g)
    arrive(1)
    edges(1)
    for g in reversed(range(PARTS // 2)):
        project_part(0, g)
    edges_in(1)
    filter_all(1)
    for g in reversed(range(PARTS)):
        project_part(1, g)
    whole(ask_ref, 1, devices, ask_sent, ask_got).wait_send()
    for h in range(2):
        whole(served.at[h], 1, devices, sent, sent).wait_send()
    loads[3].wait()
    loads[4].wait()

    lanes = lax.broadcasted_iota(jnp.int32, (8, 128), 1)
    places = lax.broadcasted_iota(jnp.int32, (8, 128), 0)
    row = jnp.zeros((8, 128), jnp.float32)
    for h in range(2):
        for i, total in enumerate(gather_up(h)):
            row = jnp.where(lanes == places * 8 + 4 * h + i, total, row)
    sums[...] = jnp.sum(row, axis=0, keepdims=True)

    def give_sums(mask):
        return remote(sums, held.at[mask], sum_sent, sum_got, place(mask))

    @functools.partial(partners)
    def _(mask):
        give_sums(mask).start()

    held[0] = sums[...]
    for h in range(2):
        these = part.at[rows_of(h, 1, others)]
        remote(these, these, back_sent, back_sent, place(1)).wait_send()
    whole(held, 1, devices, sum_sent, sum_got).wait()
    total = jnp.broadcast_to(jnp.sum(held[...], axis=0), (8, 128))
    for h in range(2):
        norm_old, curvature, cross, square = (
            jnp.take_along_axis(total, places * 8 + 4 * h + i, axis=1) for i in range(4)
        )
        step_size = norm_old / curvature
        norm_new = norm_old - step_size * (2.0 * cross - step_size * square)
        factor_ref[8 * h : 8 * h + 8, :] = jnp.where(lanes == 0, step_size, norm_new / norm_old)


def one_step(diag, patch, way, old, scale, pixels, gains, band, groups, spans):
    devices = groups * spans
    rows = pixels.shape[0]
    blocks = patch.size
    pairs = blocks // devices // 2
    tiles = way.shape[1] // 128
    edge = (2, rows // 2, 8, 128)
    both = (2, devices, pairs, 8, 128)
    flat = (2 * devices * pairs * 8, 128)
    asks = (devices, 1, 128)
    dma = pltpu.SemaphoreType.DMA
    return pl.pallas_call(
        functools.partial(step_kernel, groups, spans),
        out_shape=(
            jax.ShapeDtypeStruct(way.shape, jnp.float32),
            jax.ShapeDtypeStruct((way.shape[0], 128), jnp.float32),
        ),
        in_specs=smem(1) + vmem(1) + [pl.BlockSpec(memory_space=pltpu.HBM)] * 5 + vmem(1),
        out_specs=tuple(vmem(2)),
        scratch_shapes=[
            pltpu.VMEM(way.shape, jnp.float32),
            pltpu.VMEM(old.shape, jnp.float32),
            pltpu.VMEM(scale.shape, jnp.float32),
            pltpu.VMEM(pixels.shape, jnp.int32),
            pltpu.VMEM(gains.shape, jnp.float32),
            pltpu.SMEM((1, blocks), jnp.int32),
            pltpu.SMEM((1, blocks), jnp.int32),
            pltpu.VMEM((1, blocks), jnp.int32),
            pltpu.VMEM((1, blocks), jnp.int32),
            pltpu.VMEM(asks, jnp.int32),
            pltpu.SMEM(asks, jnp.int32),
            pltpu.VMEM(asks, jnp.int32),
            pltpu.VMEM((2, 2, tiles, 8, 128), jnp.float32),
            pltpu.VMEM(both, jnp.float32),
            pltpu.VMEM(both, jnp.float32),
            pltpu.VMEM((blocks, 128), jnp.int32),
            pltpu.VMEM((blocks, 128), jnp.int32),
            pltpu.VMEM((blocks, 128), jnp.float32),
            pltpu.VMEM((blocks, 128), jnp.float32),
            pltpu.VMEM((2, blocks, 8, 128), jnp.float32),
            pltpu.VMEM((rows, 256, 256), jnp.bfloat16),
            pltpu.VMEM((blocks, PX, 128), jnp.bfloat16),
            pltpu.VMEM(edge, jnp.float32),
            pltpu.VMEM(edge, jnp.float32),
            pltpu.VMEM(edge, jnp.float32),
            pltpu.VMEM(edge, jnp.float32),
            pltpu.VMEM((2, blocks, 16, 128), jnp.bfloat16),
            pltpu.VMEM(flat, jnp.float32),
            pltpu.VMEM(flat, jnp.float32),
            pltpu.VMEM((2 * tiles, blocks), jnp.bfloat16),
            pltpu.VMEM((2 * tiles * 8, 128), jnp.float32),
            pltpu.VMEM((1, 128), jnp.float32),
            pltpu.VMEM((devices, 1, 128), jnp.float32),
            dma((5,)),
            dma,
            dma,
            dma,
            dma((2,)),
            dma,
            dma((2, PARTS)),
            dma((2, 2)),
            dma((2, 2)),
            dma,
            dma((2, PARTS)),
            dma,
            dma,
        ],
        compiler_params=pltpu.CompilerParams(
            collective_id=0, has_side_effects=True, vmem_limit_bytes=62 * 1024 * 1024
        ),
    )(diag, patch, way, old, scale, pixels, gains, band)


def per_device(
    iterate, residual, direction, precond, patch_ids, pixel_in, weights, filter_diag, filter_band
):
    groups, spans = lax.axis_size("det"), lax.axis_size("tm")
    image_map, factor = one_step(
        filter_diag, patch_ids.T, direction, residual, precond[None, :],
        pixel_in, weights, filter_band, groups, spans,
    )
    step_size, ratio = factor[:, 0:1], factor[:, 1:2]
    new_iterate = iterate + step_size * direction
    new_residual = residual - step_size * image_map
    new_direction = precond * new_residual + ratio * direction
    return (new_iterate, new_residual, new_direction)


def solution(mesh):
    in_specs = (
        P(None, ("det", "tm")),
        P(None, ("det", "tm")),
        P(None, ("det", "tm")),
        P(("det", "tm")),
        P("det", "tm"),
        P("det", "tm"),
        P("det", "tm"),
        P("det"),
        P("det", None),
    )
    out_specs = (P(None, ("det", "tm")), P(None, ("det", "tm")), P(None, ("det", "tm")))
    return jax.shard_map(
        per_device, mesh=mesh, in_specs=in_specs, out_specs=out_specs, check_vma=False
    )
```

```python
import functools

import jax
import jax.numpy as jnp
from jax import lax
from jax.experimental import pallas as pl
from jax.experimental.pallas import tpu as pltpu
from jax.sharding import PartitionSpec as P

PX = 64
MESH = pl.DeviceIdType.MESH


def halves(values):
    top = values.astype(jnp.bfloat16)
    return top, (values - top.astype(jnp.float32)).astype(jnp.bfloat16)


PARTS = 8


def vmem(count):
    return [pl.BlockSpec(memory_space=pltpu.VMEM)] * count


def partners_of(groups, spans):
    group, span = lax.axis_index("det"), lax.axis_index("tm")
    me = group * spans + span
    shift = spans.bit_length() - 1

    def place(mask):
        return (group ^ (mask >> shift), span ^ (mask & (spans - 1)))

    return me, group, span, place


def remote(src, dst, sent, got, device):
    return pltpu.make_async_remote_copy(
        src_ref=src, dst_ref=dst, send_sem=sent, recv_sem=got, device_id=device, device_id_type=MESH
    )


def step_kernel(
    groups, spans,
    diag_hbm, patch_hbm, way_hbm, old_hbm, scale_hbm, pixel_hbm, gain_hbm, band_hbm,
    image_ref, factor_ref,
    diag_ref, patch_ref, band_ref, way_ref, old_ref, scale_ref, pixel_ref, gain_ref,
    slot_ref, block_ref, slots, listed, ask_ref, numbers, asked, table, served, patches, pixels, turned, gains, turned_gains, line, bands, hot,
    head, tail, before, after, cells, part, collected, spread, image, sums, held,
    load_sem, ask_sent, ask_got, local, list_sem, sent, got, edge_sent, edge_got, back_sent, back_got,
    sum_sent, sum_got,
):
    devices = groups * spans
    me, group, span, place = partners_of(groups, spans)
    rows = pixel_ref.shape[0]
    blocks = block_ref.shape[1]
    per_row = blocks // rows
    per_owner = blocks // devices
    pairs = per_owner // 2
    half = rows // 2
    tiles = way_ref.shape[1] // 128
    deep = pairs * 8
    others = devices - 1
    width = devices // PARTS
    left = lax.broadcasted_iota(jnp.int32, (8, 128), 1) < 64

    loads = [
        pltpu.make_async_copy(src, dst, load_sem.at[i])
        for i, (src, dst) in enumerate(
            [(way_hbm, way_ref), (pixel_hbm, pixel_ref), (gain_hbm, gain_ref), (old_hbm, old_ref), (scale_hbm, scale_ref),
             (band_hbm, band_ref), (diag_hbm, diag_ref), (patch_hbm, patch_ref)]
        )
    ]
    barrier = pltpu.get_barrier_semaphore()

    def partners(run):
        @pl.loop(0, others)
        def _(n):
            run(others - n)

    @functools.partial(partners)
    def _(mask):
        pl.semaphore_signal(barrier, inc=1, device_id=place(mask), device_id_type=MESH)

    for load in reversed(loads):
        load.start()

    lane8 = lax.broadcasted_iota(jnp.int32, (8, 128), 1)
    row8 = lax.broadcasted_iota(jnp.int32, (8, 128), 0)
    lane1 = lax.broadcasted_iota(jnp.int32, (1, 128), 1)
    square_row = lax.broadcasted_iota(jnp.int32, (128, 128), 0)
    square_lane = lax.broadcasted_iota(jnp.int32, (128, 128), 1)
    own_patches = 2 * tiles
    own_shift = own_patches.bit_length() - 1
    row_shift = rows.bit_length() - 1
    chunks = range(blocks // 128)

    def as_column(row):
        return jnp.broadcast_to(row, (128, 128)).T

    def down(values):
        return jnp.sum(values, axis=0, keepdims=True)

    loads[7].wait()
    padded = jnp.concatenate([patch_ref[...], jnp.zeros((per_row, 128 - rows), jnp.int32)], axis=1)
    repeated = jnp.take_along_axis(padded, lane8 & (rows - 1), axis=1)
    lies = [
        down(jnp.where(row8 == k * (128 // rows) + (lane8 >> row_shift), repeated, 0)) for k in chunks
    ]
    owners = [jnp.right_shift(lie, own_shift) for lie in lies]
    packed = [
        (((lane1 & (rows - 1)) * per_row + k * (128 // rows) + (lane1 >> row_shift)) << own_shift)
        + (lies[k] & (own_patches - 1))
        for k in chunks
    ]
    owner_columns = [as_column(owner) for owner in owners]
    packed_columns = [as_column(pack) for pack in packed]
    slot_rows = []
    for k in chunks:
        rank = jnp.zeros((128, 128), jnp.int32)
        for c in chunks:
            same = (owner_columns[c] == owners[k]) & (square_row + 128 * c < square_lane + 128 * k)
            rank = rank + jnp.where(same, 1, 0)
        slot_rows.append(owners[k] * per_owner + down(rank))
        slots[:, 128 * k : 128 * k + 128] = slot_rows[k] & (blocks - 1)
    slot_columns = [as_column(row) for row in slot_rows]
    for k in chunks:
        found = jnp.zeros((128, 128), jnp.int32)
        for c in chunks:
            found = found + jnp.where(slot_columns[c] == square_lane + 128 * k, packed_columns[c], 0)
        by_slot = down(found)
        listed[:, 128 * k : 128 * k + 128] = jnp.right_shift(by_slot, own_shift) & (blocks - 1)
        wide = jnp.broadcast_to(by_slot & (own_patches - 1), (8, 128))
        for p in range(128 // per_owner):
            turn = (128 - p * per_owner) % 128
            ask_ref[k * (128 // per_owner) + p] = (pltpu.roll(wide, turn, 1) if turn else wide)[:1]
    lists = [
        pltpu.make_async_copy(slots, slot_ref, list_sem.at[0]),
        pltpu.make_async_copy(listed, block_ref, list_sem.at[1]),
    ]
    for copy in lists:
        copy.start()
    asked[0] = ask_ref[me]
    pl.semaphore_wait(barrier, others)

    def ask(mask):
        return remote(ask_ref.at[me ^ mask], asked.at[mask], ask_sent, ask_got, place(mask))

    def give(h, mask):
        return remote(
            served.at[h, mask], patches.at[h, mask], sent, got.at[h, mask // width], place(mask)
        )

    def whole(ref, low, high, sent_sem, got_sem):
        these = ref.at[pl.ds(low, high - low)]
        return remote(these, these, sent_sem, got_sem, place(1))

    @functools.partial(partners)
    def _(mask):
        ask(mask).start()

    loads[0].wait()

    @pl.loop(0, tiles, unroll=2)
    def _(q):
        for h in range(2):
            tile = way_ref[8 * h : 8 * h + 8, pl.ds(pl.multiple_of(q * 128, 128), 128)]
            table[0, h, q] = tile
            table[1, h, q] = pltpu.roll(tile, 64, 1)

    whole(asked, 1, devices, ask_sent, ask_got).wait_recv()
    move = pltpu.make_async_copy(asked, numbers, local)
    move.start()
    move.wait()

    def serve(h, mask, dst):
        for i in range(pairs):
            a, b = numbers[mask, 0, 2 * i], numbers[mask, 0, 2 * i + 1]
            dst[h, mask, i] = jnp.where(left, table[a & 1, h, a >> 1], table[1 - (b & 1), h, b >> 1])

    def part_of(g):
        return max(1, g * width), (g + 1) * width

    def offer(h, g):
        low, high = part_of(g)

        @pl.loop(low, high)
        def _(mask):
            serve(h, mask, served)
            give(h, mask).start()

    for g in reversed(range(PARTS)):
        offer(0, g)
    for h in range(2):
        serve(h, 0, patches)

    loads[1].wait()
    loads[2].wait()
    for r in range(0, rows, 8):
        for j in range(per_row):
            these = pl.ds(r * per_row + j, 8, stride=per_row)
            pixel = pixel_ref[r : r + 8, 128 * j : 128 * j + 128]
            gain = gain_ref[r : r + 8, 128 * j : 128 * j + 128]
            pixels[these, :] = pixel
            turned[these, :] = pltpu.roll(pixel, 64, 1)
            gains[these, :] = gain
            turned_gains[these, :] = pltpu.roll(gain, 64, 1)

    for copy in lists:
        copy.wait()

    lane = lax.broadcasted_iota(jnp.int32, (1, 128), 1)
    loads[5].wait()
    loads[6].wait()
    band = jnp.concatenate([band_ref[...], jnp.zeros((rows, 128 - band_ref.shape[1]), jnp.float32)], axis=1)
    wanted = jnp.broadcast_to(jnp.where(lane < 64, 63 - lane, jnp.maximum(lane - 65, 0)), (rows, 128))
    upper = jnp.take_along_axis(band, wanted, axis=1)
    lower = jnp.where(
        lane == 0, jnp.take_along_axis(band, jnp.full((rows, 128), 63, jnp.int32), axis=1), 0.0
    )
    held_bands = jnp.concatenate([lower, upper], axis=1)

    wide_lane = lax.broadcasted_iota(jnp.int32, (1, 256), 1)
    for d in range(rows):
        base = jnp.where(wide_lane == 192, diag_ref[d], held_bands[d : d + 1])
        around = pltpu.roll(jnp.broadcast_to(base, (128, 256)), 0, 1, stride=1, stride_axis=0)
        bands[d] = jnp.concatenate(
            [
                jnp.concatenate(halves(around[:, :128]), axis=1),
                jnp.concatenate(halves(around[:, 128:]), axis=1),
            ],
            axis=0,
        )

    spot = lax.broadcasted_iota(jnp.int32, (PX, 128), 0)

    @pl.loop(0, blocks, unroll=2)
    def _(s):
        pixel = jnp.broadcast_to(pixels[pl.ds(block_ref[0, s], 1), :], (PX, 128))
        hot[s] = jnp.where(spot == pixel, 1.0, 0.0).astype(jnp.bfloat16)

    asks = asked[:, 0, :]
    even = jnp.concatenate(
        [jnp.broadcast_to(asks[:, 2 * i : 2 * i + 1], (devices, 2 * tiles)) for i in range(pairs)], axis=0
    )
    odd = jnp.concatenate(
        [jnp.broadcast_to(asks[:, 2 * i + 1 : 2 * i + 2], (devices, 2 * tiles)) for i in range(pairs)], axis=0
    )
    column = lax.broadcasted_iota(jnp.int32, even.shape, 1)
    first = column < tiles
    target = jnp.where(first, 2 * column, 2 * (column - tiles) + 1)
    straight = jnp.where(jnp.where(first, even, odd) == target, 1.0, 0.0)
    crossed = jnp.where(jnp.where(first, odd, even) == target, 1.0, 0.0)
    spread[...] = jnp.concatenate([straight.T, crossed.T], axis=1).astype(jnp.bfloat16)

    def scan(h, mask):
        for i in range(pairs):
            patch = patches[h, mask, i]
            for side in range(2):
                s = (me ^ mask) * per_owner + 2 * i + side
                b = block_ref[0, s]
                pixel = jnp.broadcast_to(turned[pl.ds(b, 1), :], (8, 128)) + 64 * side
                gain = jnp.broadcast_to(turned_gains[pl.ds(b, 1), :], (8, 128))
                line[h, s] = jnp.take_along_axis(patch, pixel, axis=1) * gain

    def arrive(h):
        scan(h, 0)
        for g in reversed(range(PARTS)):
            low, high = part_of(g)
            whole(patches.at[h], low, high, sent, got.at[h, g]).wait_recv()
            if h == 0 and PARTS // 2 <= g < PARTS - 1:
                offer(1, g + 1)
                if g == PARTS // 2:
                    offer(1, g)

            @pl.loop(low, high, unroll=2)
            def _(mask):
                scan(h, mask)


    forth = [
        remote(tail.at[h], before.at[h], edge_sent.at[h, 0], edge_got.at[h, 0],
               (group, lax.rem(span + 1, spans)))
        for h in range(2)
    ]
    back = [
        remote(head.at[h], after.at[h], edge_sent.at[h, 1], edge_got.at[h, 1],
               (group, lax.rem(span + spans - 1, spans)))
        for h in range(2)
    ]

    def edges(h):
        @pl.loop(0, half)
        def _(d):
            start, end = d, d + (per_row - 1) * rows
            head[h, d] = jnp.where(
                left, pltpu.roll(line[h, slot_ref[0, start]], 64, 1), line[h, slot_ref[0, start + half]]
            )
            tail[h, d] = jnp.where(
                left, line[h, slot_ref[0, end]], pltpu.roll(line[h, slot_ref[0, end + half]], 64, 1)
            )

        forth[h].start()
        back[h].start()

    def edges_in(h):
        forth[h].wait()
        back[h].wait()

        @pl.when(span == 0)
        def _():
            before[h] = jnp.zeros_like(before[h])

        @pl.when(span == spans - 1)
        def _():
            after[h] = jnp.zeros_like(after[h])

    def one_row(h, d, early, late):
        mine = [early] + [line[h, slot_ref[0, j * rows + d]] for j in range(per_row)] + [late]
        shifted = [jnp.where(left, mine[m], mine[m + 1]) for m in range(per_row + 1)]
        near = jnp.concatenate(shifted[:-1], axis=0)
        far = jnp.concatenate(shifted[1:], axis=0)
        wide = jnp.concatenate(
            [jnp.concatenate(halves(near), axis=0), jnp.concatenate(halves(far), axis=0)], axis=1
        )
        made = jnp.dot(wide, bands[d], preferred_element_type=jnp.float32)
        n = 8 * per_row
        filtered = made[:n, :128] + (made[n:, :128] + made[:n, 128:])
        for j in range(per_row):
            gain = jnp.broadcast_to(gains[pl.ds(d * per_row + j, 1), :], (8, 128))
            values = filtered[8 * j : 8 * j + 8] * gain
            top = values.astype(jnp.bfloat16).astype(jnp.float32)
            cells[h, d * per_row + j] = jnp.concatenate([top, values - top], axis=0).astype(jnp.bfloat16)

    def filter_all(h):
        @pl.loop(0, half, unroll=2)
        def _(d):
            early, late = before[h, d], after[h, d]
            one_row(h, d, early, pltpu.roll(late, 64, 1))
            one_row(h, d + half, pltpu.roll(early, 64, 1), late)

    blank = jnp.zeros((PX, 128), jnp.bfloat16)

    def project(h, mask, dst):
        for i in range(pairs):
            s = (me ^ mask) * per_owner + 2 * i
            both = jnp.concatenate([cells[h, block_ref[0, s]], cells[h, block_ref[0, s + 1]]], axis=1)
            grid = jnp.concatenate(
                [
                    jnp.concatenate([hot[s], blank], axis=1),
                    jnp.concatenate([blank, hot[s + 1]], axis=1),
                ],
                axis=0,
            )
            added = lax.dot_general(
                both, grid, (((1,), (1,)), ((), ())), preferred_element_type=jnp.float32
            )
            where = (h * devices + mask) * deep + 8 * i
            dst[pl.ds(pl.multiple_of(where, 8), 8), :] = added[:8] + added[8:]

    def rows_of(h, mask, count):
        return pl.ds(pl.multiple_of((h * devices + mask) * deep, 8), count * deep)

    def send_back(h, mask):
        these = rows_of(h, mask, 1)
        return remote(
            part.at[these], collected.at[these], back_sent, back_got.at[h, mask // width], place(mask)
        )

    def project_part(h, g):
        low, high = part_of(g)

        @pl.loop(low, high, unroll=min(8, high - low))
        def _(mask):
            project(h, mask, part)

        @pl.loop(low, high)
        def _(mask):
            send_back(h, mask).start()

        if g == 0:
            project(h, 0, collected)

    def gather_up(h):
        for g in reversed(range(PARTS)):
            low, high = part_of(g)
            these = collected.at[rows_of(h, low, high - low)]
            remote(these, these, back_sent, back_got.at[h, g], place(1)).wait_recv()

        wide_left = lax.broadcasted_iota(jnp.int32, (tiles, 128), 1) < 64
        for k in range(8):
            came = jnp.concatenate(
                [
                    collected[pl.ds(h * devices * deep + 8 * i + k, devices, stride=deep), :]
                    for i in range(pairs)
                ],
                axis=0,
            )
            came = jnp.concatenate([came, pltpu.roll(came, 64, 1)], axis=0)
            total = jnp.dot(
                spread[...], jnp.concatenate(halves(came), axis=1), preferred_element_type=jnp.float32
            )
            total = total[:, :128] + total[:, 128:]
            image[pl.ds(h * tiles * 8 + k, tiles, stride=8), :] = jnp.where(
                wide_left, total[:tiles], total[tiles:]
            )

        zero = jnp.zeros((8, 128), jnp.float32)

        def add(q, totals):
            these = pl.ds(pl.multiple_of(q * 128, 128), 128)
            tile = image[pl.ds(pl.multiple_of((h * tiles + q) * 8, 8), 8), :]
            image_ref[8 * h : 8 * h + 8, these] = tile
            old = old_ref[8 * h : 8 * h + 8, these]
            scale = jnp.broadcast_to(scale_ref[:, these], (8, 128))
            way = way_ref[8 * h : 8 * h + 8, these]
            lean = scale * old
            return (
                totals[0] + old * lean,
                totals[1] + way * tile,
                totals[2] + tile * lean,
                totals[3] + tile * (scale * tile),
            )

        return [
            jnp.sum(total, axis=1, keepdims=True)
            for total in lax.fori_loop(0, tiles, add, (zero,) * 4, unroll=4)
        ]

    arrive(0)
    edges(0)
    for g in reversed(range(PARTS // 2)):
        offer(1, g)
    edges_in(0)
    filter_all(0)
    for g in reversed(range(PARTS // 2, PARTS)):
        project_part(0, g)
    arrive(1)
    edges(1)
    for g in reversed(range(PARTS // 2)):
        project_part(0, g)
    edges_in(1)
    filter_all(1)
    for g in reversed(range(PARTS)):
        project_part(1, g)
    whole(ask_ref, 1, devices, ask_sent, ask_got).wait_send()
    for h in range(2):
        whole(served.at[h], 1, devices, sent, sent).wait_send()
    loads[3].wait()
    loads[4].wait()

    lanes = lax.broadcasted_iota(jnp.int32, (8, 128), 1)
    places = lax.broadcasted_iota(jnp.int32, (8, 128), 0)
    row = jnp.zeros((8, 128), jnp.float32)
    for h in range(2):
        for i, total in enumerate(gather_up(h)):
            row = jnp.where(lanes == places * 8 + 4 * h + i, total, row)
    sums[...] = jnp.sum(row, axis=0, keepdims=True)

    def give_sums(mask):
        return remote(sums, held.at[mask], sum_sent, sum_got, place(mask))

    @functools.partial(partners)
    def _(mask):
        give_sums(mask).start()

    held[0] = sums[...]
    for h in range(2):
        these = part.at[rows_of(h, 1, others)]
        remote(these, these, back_sent, back_sent, place(1)).wait_send()
    whole(held, 1, devices, sum_sent, sum_got).wait()
    total = jnp.broadcast_to(jnp.sum(held[...], axis=0), (8, 128))
    for h in range(2):
        norm_old, curvature, cross, square = (
            jnp.take_along_axis(total, places * 8 + 4 * h + i, axis=1) for i in range(4)
        )
        step_size = norm_old / curvature
        norm_new = norm_old - step_size * (2.0 * cross - step_size * square)
        factor_ref[8 * h : 8 * h + 8, :] = jnp.where(lanes == 0, step_size, norm_new / norm_old)


def stay(array):
    return pltpu.with_memory_space_constraint(array, pltpu.HBM)


def one_step(diag, patch, way, old, scale, pixels, gains, band, groups, spans):
    devices = groups * spans
    rows = pixels.shape[0]
    blocks = patch.size
    pairs = blocks // devices // 2
    tiles = way.shape[1] // 128
    edge = (2, rows // 2, 8, 128)
    both = (2, devices, pairs, 8, 128)
    flat = (2 * devices * pairs * 8, 128)
    asks = (devices, 1, 128)
    dma = pltpu.SemaphoreType.DMA
    return pl.pallas_call(
        functools.partial(step_kernel, groups, spans),
        out_shape=(
            jax.ShapeDtypeStruct(way.shape, jnp.float32),
            jax.ShapeDtypeStruct((way.shape[0], 128), jnp.float32),
        ),
        in_specs=[pl.BlockSpec(memory_space=pltpu.HBM)] * 8,
        out_specs=tuple(vmem(2)),
        scratch_shapes=[
            pltpu.SMEM(diag.shape, jnp.float32),
            pltpu.VMEM(patch.shape, jnp.int32),
            pltpu.VMEM(band.shape, jnp.float32),
            pltpu.VMEM(way.shape, jnp.float32),
            pltpu.VMEM(old.shape, jnp.float32),
            pltpu.VMEM(scale.shape, jnp.float32),
            pltpu.VMEM(pixels.shape, jnp.int32),
            pltpu.VMEM(gains.shape, jnp.float32),
            pltpu.SMEM((1, blocks), jnp.int32),
            pltpu.SMEM((1, blocks), jnp.int32),
            pltpu.VMEM((1, blocks), jnp.int32),
            pltpu.VMEM((1, blocks), jnp.int32),
            pltpu.VMEM(asks, jnp.int32),
            pltpu.SMEM(asks, jnp.int32),
            pltpu.VMEM(asks, jnp.int32),
            pltpu.VMEM((2, 2, tiles, 8, 128), jnp.float32),
            pltpu.VMEM(both, jnp.float32),
            pltpu.VMEM(both, jnp.float32),
            pltpu.VMEM((blocks, 128), jnp.int32),
            pltpu.VMEM((blocks, 128), jnp.int32),
            pltpu.VMEM((blocks, 128), jnp.float32),
            pltpu.VMEM((blocks, 128), jnp.float32),
            pltpu.VMEM((2, blocks, 8, 128), jnp.float32),
            pltpu.VMEM((rows, 256, 256), jnp.bfloat16),
            pltpu.VMEM((blocks, PX, 128), jnp.bfloat16),
            pltpu.VMEM(edge, jnp.float32),
            pltpu.VMEM(edge, jnp.float32),
            pltpu.VMEM(edge, jnp.float32),
            pltpu.VMEM(edge, jnp.float32),
            pltpu.VMEM((2, blocks, 16, 128), jnp.bfloat16),
            pltpu.VMEM(flat, jnp.float32),
            pltpu.VMEM(flat, jnp.float32),
            pltpu.VMEM((2 * tiles, blocks), jnp.bfloat16),
            pltpu.VMEM((2 * tiles * 8, 128), jnp.float32),
            pltpu.VMEM((1, 128), jnp.float32),
            pltpu.VMEM((devices, 1, 128), jnp.float32),
            dma((8,)),
            dma,
            dma,
            dma,
            dma((2,)),
            dma,
            dma((2, PARTS)),
            dma((2, 2)),
            dma((2, 2)),
            dma,
            dma((2, PARTS)),
            dma,
            dma,
        ],
        compiler_params=pltpu.CompilerParams(
            collective_id=0, has_side_effects=True, vmem_limit_bytes=32 * 1024 * 1024
        ),
    )(diag, patch, way, old, scale, pixels, gains, band)


def per_device(
    iterate, residual, direction, precond, patch_ids, pixel_in, weights, filter_diag, filter_band
):
    groups, spans = lax.axis_size("det"), lax.axis_size("tm")
    image_map, factor = one_step(
        *map(stay, (filter_diag, patch_ids.T, direction, residual, precond[None, :])),
        *map(stay, (pixel_in, weights, filter_band)), groups, spans,
    )
    step_size, ratio = factor[:, 0:1], factor[:, 1:2]
    new_iterate = iterate + step_size * direction
    new_residual = residual - step_size * image_map
    new_direction = precond * new_residual + ratio * direction
    return (new_iterate, new_residual, new_direction)


def solution(mesh):
    in_specs = (
        P(None, ("det", "tm")),
        P(None, ("det", "tm")),
        P(None, ("det", "tm")),
        P(("det", "tm")),
        P("det", "tm"),
        P("det", "tm"),
        P("det", "tm"),
        P("det"),
        P("det", None),
    )
    out_specs = (P(None, ("det", "tm")), P(None, ("det", "tm")), P(None, ("det", "tm")))
    return jax.shard_map(
        per_device, mesh=mesh, in_specs=in_specs, out_specs=out_specs, check_vma=False
    )
```

```python
import functools

import jax
import jax.numpy as jnp
from jax import lax
from jax.experimental import pallas as pl
from jax.experimental.pallas import tpu as pltpu
from jax.sharding import PartitionSpec as P

PX = 64
MESH = pl.DeviceIdType.MESH


def halves(values):
    top = values.astype(jnp.bfloat16)
    return top, (values - top.astype(jnp.float32)).astype(jnp.bfloat16)


PARTS = 8


def vmem(count):
    return [pl.BlockSpec(memory_space=pltpu.VMEM)] * count


def partners_of(groups, spans):
    group, span = lax.axis_index("det"), lax.axis_index("tm")
    me = group * spans + span
    shift = spans.bit_length() - 1

    def place(mask):
        return (group ^ (mask >> shift), span ^ (mask & (spans - 1)))

    return me, group, span, place


def remote(src, dst, sent, got, device):
    return pltpu.make_async_remote_copy(
        src_ref=src, dst_ref=dst, send_sem=sent, recv_sem=got, device_id=device, device_id_type=MESH
    )


def step_kernel(
    groups, spans,
    diag_hbm, patch_hbm, at_hbm, way_hbm, old_hbm, scale_hbm, pixel_hbm, gain_hbm, band_hbm,
    image_ref, factor_ref, at_ref,
    diag_ref, patch_ref, band_ref, way_ref, old_ref, scale_ref, pixel_ref, gain_ref,
    slot_ref, block_ref, slots, listed, ask_ref, numbers, asked, table, served, patches, pixels, turned, gains, turned_gains, line, bands, hot,
    head, tail, before, after, cells, part, collected, spread, image, sums, held,
    load_sem, ask_sent, ask_got, local, list_sem, sent, got, edge_sent, edge_got, back_sent, back_got,
    sum_sent, sum_got,
):
    devices = groups * spans
    me, group, span, place = partners_of(groups, spans)
    rows = pixel_ref.shape[0]
    blocks = block_ref.shape[1]
    per_row = blocks // rows
    per_owner = blocks // devices
    pairs = per_owner // 2
    half = rows // 2
    tiles = way_ref.shape[1] // 128
    deep = pairs * 8
    others = devices - 1
    width = devices // PARTS
    left = lax.broadcasted_iota(jnp.int32, (8, 128), 1) < 64

    loads = [
        pltpu.make_async_copy(src, dst, load_sem.at[i])
        for i, (src, dst) in enumerate(
            [(way_hbm, way_ref), (pixel_hbm, pixel_ref), (gain_hbm, gain_ref), (old_hbm, old_ref), (scale_hbm, scale_ref),
             (band_hbm, band_ref), (diag_hbm, diag_ref), (patch_hbm, patch_ref), (at_hbm, at_ref)]
        )
    ]
    barrier = pltpu.get_barrier_semaphore()

    def partners(run):
        @pl.loop(0, others)
        def _(n):
            run(others - n)

    @functools.partial(partners)
    def _(mask):
        pl.semaphore_signal(barrier, inc=1, device_id=place(mask), device_id_type=MESH)

    for i in (7, 0, 1, 2, 5, 6, 3, 4, 8):
        loads[i].start()

    lane8 = lax.broadcasted_iota(jnp.int32, (8, 128), 1)
    row8 = lax.broadcasted_iota(jnp.int32, (8, 128), 0)
    lane1 = lax.broadcasted_iota(jnp.int32, (1, 128), 1)
    square_row = lax.broadcasted_iota(jnp.int32, (128, 128), 0)
    square_lane = lax.broadcasted_iota(jnp.int32, (128, 128), 1)
    own_patches = 2 * tiles
    own_shift = own_patches.bit_length() - 1
    row_shift = rows.bit_length() - 1
    chunks = range(blocks // 128)

    def as_column(row):
        return jnp.broadcast_to(row, (128, 128)).T

    def down(values):
        return jnp.sum(values, axis=0, keepdims=True)

    loads[7].wait()
    padded = jnp.concatenate([patch_ref[...], jnp.zeros((per_row, 128 - rows), jnp.int32)], axis=1)
    repeated = jnp.take_along_axis(padded, lane8 & (rows - 1), axis=1)
    lies = [
        down(jnp.where(row8 == k * (128 // rows) + (lane8 >> row_shift), repeated, 0)) for k in chunks
    ]
    owners = [jnp.right_shift(lie, own_shift) for lie in lies]
    packed = [
        (((lane1 & (rows - 1)) * per_row + k * (128 // rows) + (lane1 >> row_shift)) << own_shift)
        + (lies[k] & (own_patches - 1))
        for k in chunks
    ]
    owner_columns = [as_column(owner) for owner in owners]
    packed_columns = [as_column(pack) for pack in packed]
    slot_rows = []
    for k in chunks:
        rank = jnp.zeros((128, 128), jnp.int32)
        for c in chunks:
            same = (owner_columns[c] == owners[k]) & (square_row + 128 * c < square_lane + 128 * k)
            rank = rank + jnp.where(same, 1, 0)
        slot_rows.append(owners[k] * per_owner + down(rank))
        slots[:, 128 * k : 128 * k + 128] = slot_rows[k] & (blocks - 1)
    slot_columns = [as_column(row) for row in slot_rows]
    for k in chunks:
        found = jnp.zeros((128, 128), jnp.int32)
        for c in chunks:
            found = found + jnp.where(slot_columns[c] == square_lane + 128 * k, packed_columns[c], 0)
        by_slot = down(found)
        listed[:, 128 * k : 128 * k + 128] = jnp.right_shift(by_slot, own_shift) & (blocks - 1)
        wide = jnp.broadcast_to(by_slot & (own_patches - 1), (8, 128))
        for p in range(128 // per_owner):
            turn = (128 - p * per_owner) % 128
            ask_ref[k * (128 // per_owner) + p] = (pltpu.roll(wide, turn, 1) if turn else wide)[:1]
    lists = [
        pltpu.make_async_copy(slots, slot_ref, list_sem.at[0]),
        pltpu.make_async_copy(listed, block_ref, list_sem.at[1]),
    ]
    for copy in lists:
        copy.start()
    asked[0] = ask_ref[me]
    pl.semaphore_wait(barrier, others)

    def ask(mask):
        return remote(ask_ref.at[me ^ mask], asked.at[mask], ask_sent, ask_got, place(mask))

    def give(h, mask):
        return remote(
            served.at[h, mask], patches.at[h, mask], sent, got.at[h, mask // width], place(mask)
        )

    def whole(ref, low, high, sent_sem, got_sem):
        these = ref.at[pl.ds(low, high - low)]
        return remote(these, these, sent_sem, got_sem, place(1))

    @functools.partial(partners)
    def _(mask):
        ask(mask).start()

    loads[0].wait()

    @pl.loop(0, tiles, unroll=2)
    def _(q):
        for h in range(2):
            tile = way_ref[8 * h : 8 * h + 8, pl.ds(pl.multiple_of(q * 128, 128), 128)]
            table[0, h, q] = tile
            table[1, h, q] = pltpu.roll(tile, 64, 1)

    whole(asked, 1, devices, ask_sent, ask_got).wait_recv()
    move = pltpu.make_async_copy(asked, numbers, local)
    move.start()
    move.wait()

    def serve(h, mask, dst):
        for i in range(pairs):
            a, b = numbers[mask, 0, 2 * i], numbers[mask, 0, 2 * i + 1]
            dst[h, mask, i] = jnp.where(left, table[a & 1, h, a >> 1], table[1 - (b & 1), h, b >> 1])

    def part_of(g):
        return max(1, g * width), (g + 1) * width

    def offer(h, g):
        low, high = part_of(g)

        @pl.loop(low, high)
        def _(mask):
            serve(h, mask, served)
            give(h, mask).start()

    for g in reversed(range(PARTS)):
        offer(0, g)
    for h in range(2):
        serve(h, 0, patches)

    loads[1].wait()
    loads[2].wait()
    for r in range(0, rows, 8):
        for j in range(per_row):
            these = pl.ds(r * per_row + j, 8, stride=per_row)
            pixel = pixel_ref[r : r + 8, 128 * j : 128 * j + 128]
            gain = gain_ref[r : r + 8, 128 * j : 128 * j + 128]
            pixels[these, :] = pixel
            turned[these, :] = pltpu.roll(pixel, 64, 1)
            gains[these, :] = gain
            turned_gains[these, :] = pltpu.roll(gain, 64, 1)

    for copy in lists:
        copy.wait()

    lane = lax.broadcasted_iota(jnp.int32, (1, 128), 1)
    loads[5].wait()
    loads[6].wait()
    band = jnp.concatenate([band_ref[...], jnp.zeros((rows, 128 - band_ref.shape[1]), jnp.float32)], axis=1)
    wanted = jnp.broadcast_to(jnp.where(lane < 64, 63 - lane, jnp.maximum(lane - 65, 0)), (rows, 128))
    upper = jnp.take_along_axis(band, wanted, axis=1)
    lower = jnp.where(
        lane == 0, jnp.take_along_axis(band, jnp.full((rows, 128), 63, jnp.int32), axis=1), 0.0
    )
    held_bands = jnp.concatenate([lower, upper], axis=1)

    wide_lane = lax.broadcasted_iota(jnp.int32, (1, 256), 1)
    for d in range(rows):
        base = jnp.where(wide_lane == 192, diag_ref[d], held_bands[d : d + 1])
        around = pltpu.roll(jnp.broadcast_to(base, (128, 256)), 0, 1, stride=1, stride_axis=0)
        bands[d] = jnp.concatenate(
            [
                jnp.concatenate(halves(around[:, :128]), axis=1),
                jnp.concatenate(halves(around[:, 128:]), axis=1),
            ],
            axis=0,
        )

    spot = lax.broadcasted_iota(jnp.int32, (PX, 128), 0)

    @pl.loop(0, blocks, unroll=2)
    def _(s):
        pixel = jnp.broadcast_to(pixels[pl.ds(block_ref[0, s], 1), :], (PX, 128))
        hot[s] = jnp.where(spot == pixel, 1.0, 0.0).astype(jnp.bfloat16)

    asks = asked[:, 0, :]
    even = jnp.concatenate(
        [jnp.broadcast_to(asks[:, 2 * i : 2 * i + 1], (devices, 2 * tiles)) for i in range(pairs)], axis=0
    )
    odd = jnp.concatenate(
        [jnp.broadcast_to(asks[:, 2 * i + 1 : 2 * i + 2], (devices, 2 * tiles)) for i in range(pairs)], axis=0
    )
    column = lax.broadcasted_iota(jnp.int32, even.shape, 1)
    first = column < tiles
    target = jnp.where(first, 2 * column, 2 * (column - tiles) + 1)
    straight = jnp.where(jnp.where(first, even, odd) == target, 1.0, 0.0)
    crossed = jnp.where(jnp.where(first, odd, even) == target, 1.0, 0.0)
    spread[...] = jnp.concatenate([straight.T, crossed.T], axis=1).astype(jnp.bfloat16)

    def scan(h, mask):
        for i in range(pairs):
            patch = patches[h, mask, i]
            for side in range(2):
                s = (me ^ mask) * per_owner + 2 * i + side
                b = block_ref[0, s]
                pixel = jnp.broadcast_to(turned[pl.ds(b, 1), :], (8, 128)) + 64 * side
                gain = jnp.broadcast_to(turned_gains[pl.ds(b, 1), :], (8, 128))
                line[h, s] = jnp.take_along_axis(patch, pixel, axis=1) * gain

    def arrive(h):
        scan(h, 0)
        for g in reversed(range(PARTS)):
            low, high = part_of(g)
            whole(patches.at[h], low, high, sent, got.at[h, g]).wait_recv()
            if h == 0 and PARTS // 2 <= g < PARTS - 1:
                offer(1, g + 1)
                if g == PARTS // 2:
                    offer(1, g)

            @pl.loop(low, high, unroll=2)
            def _(mask):
                scan(h, mask)


    forth = [
        remote(tail.at[h], before.at[h], edge_sent.at[h, 0], edge_got.at[h, 0],
               (group, lax.rem(span + 1, spans)))
        for h in range(2)
    ]
    back = [
        remote(head.at[h], after.at[h], edge_sent.at[h, 1], edge_got.at[h, 1],
               (group, lax.rem(span + spans - 1, spans)))
        for h in range(2)
    ]

    def edges(h):
        @pl.loop(0, half)
        def _(d):
            start, end = d, d + (per_row - 1) * rows
            head[h, d] = jnp.where(
                left, pltpu.roll(line[h, slot_ref[0, start]], 64, 1), line[h, slot_ref[0, start + half]]
            )
            tail[h, d] = jnp.where(
                left, line[h, slot_ref[0, end]], pltpu.roll(line[h, slot_ref[0, end + half]], 64, 1)
            )

        forth[h].start()
        back[h].start()

    def edges_in(h):
        forth[h].wait()
        back[h].wait()

        @pl.when(span == 0)
        def _():
            before[h] = jnp.zeros_like(before[h])

        @pl.when(span == spans - 1)
        def _():
            after[h] = jnp.zeros_like(after[h])

    def one_row(h, d, early, late):
        mine = [early] + [line[h, slot_ref[0, j * rows + d]] for j in range(per_row)] + [late]
        shifted = [jnp.where(left, mine[m], mine[m + 1]) for m in range(per_row + 1)]
        near = jnp.concatenate(shifted[:-1], axis=0)
        far = jnp.concatenate(shifted[1:], axis=0)
        wide = jnp.concatenate(
            [jnp.concatenate(halves(near), axis=0), jnp.concatenate(halves(far), axis=0)], axis=1
        )
        made = jnp.dot(wide, bands[d], preferred_element_type=jnp.float32)
        n = 8 * per_row
        filtered = made[:n, :128] + (made[n:, :128] + made[:n, 128:])
        for j in range(per_row):
            gain = jnp.broadcast_to(gains[pl.ds(d * per_row + j, 1), :], (8, 128))
            values = filtered[8 * j : 8 * j + 8] * gain
            top = values.astype(jnp.bfloat16).astype(jnp.float32)
            cells[h, d * per_row + j] = jnp.concatenate([top, values - top], axis=0).astype(jnp.bfloat16)

    def filter_all(h):
        @pl.loop(0, half, unroll=2)
        def _(d):
            early, late = before[h, d], after[h, d]
            one_row(h, d, early, pltpu.roll(late, 64, 1))
            one_row(h, d + half, pltpu.roll(early, 64, 1), late)

    blank = jnp.zeros((PX, 128), jnp.bfloat16)

    def project(h, mask, dst):
        for i in range(pairs):
            s = (me ^ mask) * per_owner + 2 * i
            both = jnp.concatenate([cells[h, block_ref[0, s]], cells[h, block_ref[0, s + 1]]], axis=1)
            grid = jnp.concatenate(
                [
                    jnp.concatenate([hot[s], blank], axis=1),
                    jnp.concatenate([blank, hot[s + 1]], axis=1),
                ],
                axis=0,
            )
            added = lax.dot_general(
                both, grid, (((1,), (1,)), ((), ())), preferred_element_type=jnp.float32
            )
            where = (h * devices + mask) * deep + 8 * i
            dst[pl.ds(pl.multiple_of(where, 8), 8), :] = added[:8] + added[8:]

    def rows_of(h, mask, count):
        return pl.ds(pl.multiple_of((h * devices + mask) * deep, 8), count * deep)

    def send_back(h, mask):
        these = rows_of(h, mask, 1)
        return remote(
            part.at[these], collected.at[these], back_sent, back_got.at[h, mask // width], place(mask)
        )

    def project_part(h, g):
        low, high = part_of(g)

        @pl.loop(low, high, unroll=min(8, high - low))
        def _(mask):
            project(h, mask, part)

        @pl.loop(low, high)
        def _(mask):
            send_back(h, mask).start()

        if g == 0:
            project(h, 0, collected)

    def gather_up(h):
        for g in reversed(range(PARTS)):
            low, high = part_of(g)
            these = collected.at[rows_of(h, low, high - low)]
            remote(these, these, back_sent, back_got.at[h, g], place(1)).wait_recv()

        wide_left = lax.broadcasted_iota(jnp.int32, (tiles, 128), 1) < 64
        for k in range(8):
            came = jnp.concatenate(
                [
                    collected[pl.ds(h * devices * deep + 8 * i + k, devices, stride=deep), :]
                    for i in range(pairs)
                ],
                axis=0,
            )
            came = jnp.concatenate([came, pltpu.roll(came, 64, 1)], axis=0)
            total = jnp.dot(
                spread[...], jnp.concatenate(halves(came), axis=1), preferred_element_type=jnp.float32
            )
            total = total[:, :128] + total[:, 128:]
            image[pl.ds(h * tiles * 8 + k, tiles, stride=8), :] = jnp.where(
                wide_left, total[:tiles], total[tiles:]
            )

        zero = jnp.zeros((8, 128), jnp.float32)

        def add(q, totals):
            these = pl.ds(pl.multiple_of(q * 128, 128), 128)
            tile = image[pl.ds(pl.multiple_of((h * tiles + q) * 8, 8), 8), :]
            image_ref[8 * h : 8 * h + 8, these] = tile
            old = old_ref[8 * h : 8 * h + 8, these]
            scale = jnp.broadcast_to(scale_ref[:, these], (8, 128))
            way = way_ref[8 * h : 8 * h + 8, these]
            lean = scale * old
            return (
                totals[0] + old * lean,
                totals[1] + way * tile,
                totals[2] + tile * lean,
                totals[3] + tile * (scale * tile),
            )

        return [
            jnp.sum(total, axis=1, keepdims=True)
            for total in lax.fori_loop(0, tiles, add, (zero,) * 4, unroll=4)
        ]

    arrive(0)
    edges(0)
    for g in reversed(range(PARTS // 2)):
        offer(1, g)
    edges_in(0)
    filter_all(0)
    for g in reversed(range(PARTS // 2, PARTS)):
        project_part(0, g)
    arrive(1)
    edges(1)
    for g in reversed(range(PARTS // 2)):
        project_part(0, g)
    edges_in(1)
    filter_all(1)
    for g in reversed(range(PARTS)):
        project_part(1, g)
    whole(ask_ref, 1, devices, ask_sent, ask_got).wait_send()
    for h in range(2):
        whole(served.at[h], 1, devices, sent, sent).wait_send()
    loads[3].wait()
    loads[4].wait()
    loads[8].wait()

    lanes = lax.broadcasted_iota(jnp.int32, (8, 128), 1)
    places = lax.broadcasted_iota(jnp.int32, (8, 128), 0)
    row = jnp.zeros((8, 128), jnp.float32)
    for h in range(2):
        for i, total in enumerate(gather_up(h)):
            row = jnp.where(lanes == places * 8 + 4 * h + i, total, row)
    sums[...] = jnp.sum(row, axis=0, keepdims=True)

    def give_sums(mask):
        return remote(sums, held.at[mask], sum_sent, sum_got, place(mask))

    @functools.partial(partners)
    def _(mask):
        give_sums(mask).start()

    held[0] = sums[...]
    for h in range(2):
        these = part.at[rows_of(h, 1, others)]
        remote(these, these, back_sent, back_sent, place(1)).wait_send()
    whole(held, 1, devices, sum_sent, sum_got).wait()
    total = jnp.broadcast_to(jnp.sum(held[...], axis=0), (8, 128))
    for h in range(2):
        norm_old, curvature, cross, square = (
            jnp.take_along_axis(total, places * 8 + 4 * h + i, axis=1) for i in range(4)
        )
        step_size = norm_old / curvature
        norm_new = norm_old - step_size * (2.0 * cross - step_size * square)
        factor_ref[8 * h : 8 * h + 8, :] = jnp.where(lanes == 0, step_size, norm_new / norm_old)


def stay(array):
    return pltpu.with_memory_space_constraint(array, pltpu.HBM)


def one_step(diag, patch, at, way, old, scale, pixels, gains, band, groups, spans):
    devices = groups * spans
    rows = pixels.shape[0]
    blocks = patch.size
    pairs = blocks // devices // 2
    tiles = way.shape[1] // 128
    edge = (2, rows // 2, 8, 128)
    both = (2, devices, pairs, 8, 128)
    flat = (2 * devices * pairs * 8, 128)
    asks = (devices, 1, 128)
    dma = pltpu.SemaphoreType.DMA
    return pl.pallas_call(
        functools.partial(step_kernel, groups, spans),
        out_shape=(
            jax.ShapeDtypeStruct(way.shape, jnp.float32),
            jax.ShapeDtypeStruct((way.shape[0], 128), jnp.float32),
            jax.ShapeDtypeStruct(at.shape, jnp.float32),
        ),
        in_specs=[pl.BlockSpec(memory_space=pltpu.HBM)] * 9,
        out_specs=tuple(vmem(3)),
        scratch_shapes=[
            pltpu.SMEM(diag.shape, jnp.float32),
            pltpu.VMEM(patch.shape, jnp.int32),
            pltpu.VMEM(band.shape, jnp.float32),
            pltpu.VMEM(way.shape, jnp.float32),
            pltpu.VMEM(old.shape, jnp.float32),
            pltpu.VMEM(scale.shape, jnp.float32),
            pltpu.VMEM(pixels.shape, jnp.int32),
            pltpu.VMEM(gains.shape, jnp.float32),
            pltpu.SMEM((1, blocks), jnp.int32),
            pltpu.SMEM((1, blocks), jnp.int32),
            pltpu.VMEM((1, blocks), jnp.int32),
            pltpu.VMEM((1, blocks), jnp.int32),
            pltpu.VMEM(asks, jnp.int32),
            pltpu.SMEM(asks, jnp.int32),
            pltpu.VMEM(asks, jnp.int32),
            pltpu.VMEM((2, 2, tiles, 8, 128), jnp.float32),
            pltpu.VMEM(both, jnp.float32),
            pltpu.VMEM(both, jnp.float32),
            pltpu.VMEM((blocks, 128), jnp.int32),
            pltpu.VMEM((blocks, 128), jnp.int32),
            pltpu.VMEM((blocks, 128), jnp.float32),
            pltpu.VMEM((blocks, 128), jnp.float32),
            pltpu.VMEM((2, blocks, 8, 128), jnp.float32),
            pltpu.VMEM((rows, 256, 256), jnp.bfloat16),
            pltpu.VMEM((blocks, PX, 128), jnp.bfloat16),
            pltpu.VMEM(edge, jnp.float32),
            pltpu.VMEM(edge, jnp.float32),
            pltpu.VMEM(edge, jnp.float32),
            pltpu.VMEM(edge, jnp.float32),
            pltpu.VMEM((2, blocks, 16, 128), jnp.bfloat16),
            pltpu.VMEM(flat, jnp.float32),
            pltpu.VMEM(flat, jnp.float32),
            pltpu.VMEM((2 * tiles, blocks), jnp.bfloat16),
            pltpu.VMEM((2 * tiles * 8, 128), jnp.float32),
            pltpu.VMEM((1, 128), jnp.float32),
            pltpu.VMEM((devices, 1, 128), jnp.float32),
            dma((9,)),
            dma,
            dma,
            dma,
            dma((2,)),
            dma,
            dma((2, PARTS)),
            dma((2, 2)),
            dma((2, 2)),
            dma,
            dma((2, PARTS)),
            dma,
            dma,
        ],
        compiler_params=pltpu.CompilerParams(
            collective_id=0, has_side_effects=True, vmem_limit_bytes=32 * 1024 * 1024
        ),
    )(diag, patch, at, way, old, scale, pixels, gains, band)


def per_device(
    iterate, residual, direction, precond, patch_ids, pixel_in, weights, filter_diag, filter_band
):
    groups, spans = lax.axis_size("det"), lax.axis_size("tm")
    image_map, factor, kept = one_step(
        *map(stay, (filter_diag, patch_ids.T, iterate, direction, residual, precond[None, :])),
        *map(stay, (pixel_in, weights, filter_band)), groups, spans,
    )
    step_size, ratio = factor[:, 0:1], factor[:, 1:2]
    new_iterate = kept + step_size * direction
    new_residual = residual - step_size * image_map
    new_direction = precond * new_residual + ratio * direction
    return (new_iterate, new_residual, new_direction)


def solution(mesh):
    in_specs = (
        P(None, ("det", "tm")),
        P(None, ("det", "tm")),
        P(None, ("det", "tm")),
        P(("det", "tm")),
        P("det", "tm"),
        P("det", "tm"),
        P("det", "tm"),
        P("det"),
        P("det", None),
    )
    out_specs = (P(None, ("det", "tm")), P(None, ("det", "tm")), P(None, ("det", "tm")))
    return jax.shard_map(
        per_device, mesh=mesh, in_specs=in_specs, out_specs=out_specs, check_vma=False
    )
```

```python
import functools

import jax
import jax.numpy as jnp
from jax import lax
from jax.experimental import pallas as pl
from jax.experimental.pallas import tpu as pltpu
from jax.sharding import PartitionSpec as P

PX = 64
MESH = pl.DeviceIdType.MESH


def halves(values):
    top = values.astype(jnp.bfloat16)
    return top, (values - top.astype(jnp.float32)).astype(jnp.bfloat16)


PARTS = 8


def vmem(count):
    return [pl.BlockSpec(memory_space=pltpu.VMEM)] * count


def partners_of(groups, spans):
    group, span = lax.axis_index("det"), lax.axis_index("tm")
    me = group * spans + span
    shift = spans.bit_length() - 1

    def place(mask):
        return (group ^ (mask >> shift), span ^ (mask & (spans - 1)))

    return me, group, span, place


def remote(src, dst, sent, got, device):
    return pltpu.make_async_remote_copy(
        src_ref=src, dst_ref=dst, send_sem=sent, recv_sem=got, device_id=device, device_id_type=MESH
    )


def step_kernel(
    groups, spans,
    diag_hbm, patch_hbm, at_hbm, way_hbm, old_hbm, scale_hbm, pixel_hbm, gain_hbm, band_hbm,
    image_ref, factor_ref, at_ref,
    diag_ref, patch_ref, band_ref, way_ref, old_ref, scale_ref, pixel_ref, gain_ref,
    slot_ref, block_ref, slots, listed, ask_ref, numbers, asked, table, served, patches, pixels, turned, gains, turned_gains, line, bands, hot,
    head, tail, before, after, cells, part, collected, spread, image, lean_ref, sums, held,
    load_sem, ask_sent, ask_got, local, list_sem, sent, got, edge_sent, edge_got, back_sent, back_got,
    sum_sent, sum_got,
):
    devices = groups * spans
    me, group, span, place = partners_of(groups, spans)
    rows = pixel_ref.shape[0]
    blocks = block_ref.shape[1]
    per_row = blocks // rows
    per_owner = blocks // devices
    pairs = per_owner // 2
    half = rows // 2
    tiles = way_ref.shape[1] // 128
    deep = pairs * 8
    others = devices - 1
    width = devices // PARTS
    left = lax.broadcasted_iota(jnp.int32, (8, 128), 1) < 64

    loads = [
        pltpu.make_async_copy(src, dst, load_sem.at[i])
        for i, (src, dst) in enumerate(
            [(way_hbm, way_ref), (pixel_hbm, pixel_ref), (gain_hbm, gain_ref), (old_hbm, old_ref), (scale_hbm, scale_ref),
             (band_hbm, band_ref), (diag_hbm, diag_ref), (patch_hbm, patch_ref), (at_hbm, at_ref)]
        )
    ]
    barrier = pltpu.get_barrier_semaphore()

    def partners(run):
        @pl.loop(0, others)
        def _(n):
            run(others - n)

    @functools.partial(partners)
    def _(mask):
        pl.semaphore_signal(barrier, inc=1, device_id=place(mask), device_id_type=MESH)

    for i in (7, 0, 1, 2, 5, 6, 3, 4, 8):
        loads[i].start()

    lane8 = lax.broadcasted_iota(jnp.int32, (8, 128), 1)
    row8 = lax.broadcasted_iota(jnp.int32, (8, 128), 0)
    lane1 = lax.broadcasted_iota(jnp.int32, (1, 128), 1)
    square_row = lax.broadcasted_iota(jnp.int32, (128, 128), 0)
    square_lane = lax.broadcasted_iota(jnp.int32, (128, 128), 1)
    own_patches = 2 * tiles
    own_shift = own_patches.bit_length() - 1
    row_shift = rows.bit_length() - 1
    chunks = range(blocks // 128)

    def as_column(row):
        return jnp.broadcast_to(row, (128, 128)).T

    def down(values):
        return jnp.sum(values, axis=0, keepdims=True)

    loads[7].wait()
    padded = jnp.concatenate([patch_ref[...], jnp.zeros((per_row, 128 - rows), jnp.int32)], axis=1)
    repeated = jnp.take_along_axis(padded, lane8 & (rows - 1), axis=1)
    lies = [
        down(jnp.where(row8 == k * (128 // rows) + (lane8 >> row_shift), repeated, 0)) for k in chunks
    ]
    owners = [jnp.right_shift(lie, own_shift) for lie in lies]
    packed = [
        (((lane1 & (rows - 1)) * per_row + k * (128 // rows) + (lane1 >> row_shift)) << own_shift)
        + (lies[k] & (own_patches - 1))
        for k in chunks
    ]
    owner_columns = [as_column(owner) for owner in owners]
    packed_columns = [as_column(pack) for pack in packed]
    slot_rows = []
    for k in chunks:
        rank = jnp.zeros((128, 128), jnp.int32)
        for c in chunks:
            same = (owner_columns[c] == owners[k]) & (square_row + 128 * c < square_lane + 128 * k)
            rank = rank + jnp.where(same, 1, 0)
        slot_rows.append(owners[k] * per_owner + down(rank))
        slots[:, 128 * k : 128 * k + 128] = slot_rows[k] & (blocks - 1)
    slot_columns = [as_column(row) for row in slot_rows]
    for k in chunks:
        found = jnp.zeros((128, 128), jnp.int32)
        for c in chunks:
            found = found + jnp.where(slot_columns[c] == square_lane + 128 * k, packed_columns[c], 0)
        by_slot = down(found)
        listed[:, 128 * k : 128 * k + 128] = jnp.right_shift(by_slot, own_shift) & (blocks - 1)
        wide = jnp.broadcast_to(by_slot & (own_patches - 1), (8, 128))
        for p in range(128 // per_owner):
            turn = (128 - p * per_owner) % 128
            ask_ref[k * (128 // per_owner) + p] = (pltpu.roll(wide, turn, 1) if turn else wide)[:1]
    lists = [
        pltpu.make_async_copy(slots, slot_ref, list_sem.at[0]),
        pltpu.make_async_copy(listed, block_ref, list_sem.at[1]),
    ]
    for copy in lists:
        copy.start()
    asked[0] = ask_ref[me]
    pl.semaphore_wait(barrier, others)

    def ask(mask):
        return remote(ask_ref.at[me ^ mask], asked.at[mask], ask_sent, ask_got, place(mask))

    def give(h, mask):
        return remote(
            served.at[h, mask], patches.at[h, mask], sent, got.at[h, mask // width], place(mask)
        )

    def whole(ref, low, high, sent_sem, got_sem):
        these = ref.at[pl.ds(low, high - low)]
        return remote(these, these, sent_sem, got_sem, place(1))

    @functools.partial(partners)
    def _(mask):
        ask(mask).start()

    loads[0].wait()

    @pl.loop(0, tiles, unroll=2)
    def _(q):
        for h in range(2):
            tile = way_ref[8 * h : 8 * h + 8, pl.ds(pl.multiple_of(q * 128, 128), 128)]
            table[0, h, q] = tile
            table[1, h, q] = pltpu.roll(tile, 64, 1)

    whole(asked, 1, devices, ask_sent, ask_got).wait_recv()
    move = pltpu.make_async_copy(asked, numbers, local)
    move.start()
    move.wait()

    def serve(h, mask, dst):
        for i in range(pairs):
            a, b = numbers[mask, 0, 2 * i], numbers[mask, 0, 2 * i + 1]
            dst[h, mask, i] = jnp.where(left, table[a & 1, h, a >> 1], table[1 - (b & 1), h, b >> 1])

    def part_of(g):
        return max(1, g * width), (g + 1) * width

    def offer(h, g):
        low, high = part_of(g)

        @pl.loop(low, high)
        def _(mask):
            serve(h, mask, served)
            give(h, mask).start()

    for g in reversed(range(PARTS)):
        offer(0, g)
    for h in range(2):
        serve(h, 0, patches)

    loads[1].wait()
    loads[2].wait()
    for r in range(0, rows, 8):
        for j in range(per_row):
            these = pl.ds(r * per_row + j, 8, stride=per_row)
            pixel = pixel_ref[r : r + 8, 128 * j : 128 * j + 128]
            gain = gain_ref[r : r + 8, 128 * j : 128 * j + 128]
            pixels[these, :] = pixel
            turned[these, :] = pltpu.roll(pixel, 64, 1)
            gains[these, :] = gain
            turned_gains[these, :] = pltpu.roll(gain, 64, 1)

    for copy in lists:
        copy.wait()

    lane = lax.broadcasted_iota(jnp.int32, (1, 128), 1)
    loads[5].wait()
    loads[6].wait()
    band = jnp.concatenate([band_ref[...], jnp.zeros((rows, 128 - band_ref.shape[1]), jnp.float32)], axis=1)
    wanted = jnp.broadcast_to(jnp.where(lane < 64, 63 - lane, jnp.maximum(lane - 65, 0)), (rows, 128))
    upper = jnp.take_along_axis(band, wanted, axis=1)
    lower = jnp.where(
        lane == 0, jnp.take_along_axis(band, jnp.full((rows, 128), 63, jnp.int32), axis=1), 0.0
    )
    held_bands = jnp.concatenate([lower, upper], axis=1)

    wide_lane = lax.broadcasted_iota(jnp.int32, (1, 256), 1)
    for d in range(rows):
        base = jnp.where(wide_lane == 192, diag_ref[d], held_bands[d : d + 1])
        around = pltpu.roll(jnp.broadcast_to(base, (128, 256)), 0, 1, stride=1, stride_axis=0)
        bands[d] = jnp.concatenate(
            [
                jnp.concatenate(halves(around[:, :128]), axis=1),
                jnp.concatenate(halves(around[:, 128:]), axis=1),
            ],
            axis=0,
        )

    spot = lax.broadcasted_iota(jnp.int32, (PX, 128), 0)

    @pl.loop(0, blocks, unroll=2)
    def _(s):
        pixel = jnp.broadcast_to(pixels[pl.ds(block_ref[0, s], 1), :], (PX, 128))
        hot[s] = jnp.where(spot == pixel, 1.0, 0.0).astype(jnp.bfloat16)

    asks = asked[:, 0, :]
    even = jnp.concatenate(
        [jnp.broadcast_to(asks[:, 2 * i : 2 * i + 1], (devices, 2 * tiles)) for i in range(pairs)], axis=0
    )
    odd = jnp.concatenate(
        [jnp.broadcast_to(asks[:, 2 * i + 1 : 2 * i + 2], (devices, 2 * tiles)) for i in range(pairs)], axis=0
    )
    column = lax.broadcasted_iota(jnp.int32, even.shape, 1)
    first = column < tiles
    target = jnp.where(first, 2 * column, 2 * (column - tiles) + 1)
    straight = jnp.where(jnp.where(first, even, odd) == target, 1.0, 0.0)
    crossed = jnp.where(jnp.where(first, odd, even) == target, 1.0, 0.0)
    spread[...] = jnp.concatenate([straight.T, crossed.T] * 2, axis=1).astype(jnp.bfloat16)

    def scan(h, mask):
        for i in range(pairs):
            patch = patches[h, mask, i]
            for side in range(2):
                s = (me ^ mask) * per_owner + 2 * i + side
                b = block_ref[0, s]
                pixel = jnp.broadcast_to(turned[pl.ds(b, 1), :], (8, 128)) + 64 * side
                gain = jnp.broadcast_to(turned_gains[pl.ds(b, 1), :], (8, 128))
                line[h, s] = jnp.take_along_axis(patch, pixel, axis=1) * gain

    def arrive(h):
        scan(h, 0)
        for g in reversed(range(PARTS)):
            low, high = part_of(g)
            whole(patches.at[h], low, high, sent, got.at[h, g]).wait_recv()
            if h == 0 and PARTS // 2 <= g < PARTS - 1:
                offer(1, g + 1)
                if g == PARTS // 2:
                    offer(1, g)
                    for later in reversed(range(PARTS // 2)):
                        offer(1, later)

            @pl.loop(low, high, unroll=2)
            def _(mask):
                scan(h, mask)


    forth = [
        remote(tail.at[h], before.at[h], edge_sent.at[h, 0], edge_got.at[h, 0],
               (group, lax.rem(span + 1, spans)))
        for h in range(2)
    ]
    back = [
        remote(head.at[h], after.at[h], edge_sent.at[h, 1], edge_got.at[h, 1],
               (group, lax.rem(span + spans - 1, spans)))
        for h in range(2)
    ]

    def edges(h):
        @pl.loop(0, half)
        def _(d):
            start, end = d, d + (per_row - 1) * rows
            head[h, d] = jnp.where(
                left, pltpu.roll(line[h, slot_ref[0, start]], 64, 1), line[h, slot_ref[0, start + half]]
            )
            tail[h, d] = jnp.where(
                left, line[h, slot_ref[0, end]], pltpu.roll(line[h, slot_ref[0, end + half]], 64, 1)
            )

        forth[h].start()
        back[h].start()

    def edges_in(h):
        forth[h].wait()
        back[h].wait()

        @pl.when(span == 0)
        def _():
            before[h] = jnp.zeros_like(before[h])

        @pl.when(span == spans - 1)
        def _():
            after[h] = jnp.zeros_like(after[h])

    def one_row(h, d, early, late):
        mine = [early] + [line[h, slot_ref[0, j * rows + d]] for j in range(per_row)] + [late]
        shifted = [jnp.where(left, mine[m], mine[m + 1]) for m in range(per_row + 1)]
        near = jnp.concatenate(shifted[:-1], axis=0)
        far = jnp.concatenate(shifted[1:], axis=0)
        wide = jnp.concatenate(
            [jnp.concatenate(halves(near), axis=0), jnp.concatenate(halves(far), axis=0)], axis=1
        )
        made = jnp.dot(wide, bands[d], preferred_element_type=jnp.float32)
        n = 8 * per_row
        filtered = made[:n, :128] + (made[n:, :128] + made[:n, 128:])
        for j in range(per_row):
            gain = jnp.broadcast_to(gains[pl.ds(d * per_row + j, 1), :], (8, 128))
            values = filtered[8 * j : 8 * j + 8] * gain
            top = values.astype(jnp.bfloat16).astype(jnp.float32)
            cells[h, d * per_row + j] = jnp.concatenate([top, values - top], axis=0).astype(jnp.bfloat16)

    def filter_all(h):
        @pl.loop(0, half, unroll=2)
        def _(d):
            early, late = before[h, d], after[h, d]
            one_row(h, d, early, pltpu.roll(late, 64, 1))
            one_row(h, d + half, pltpu.roll(early, 64, 1), late)

    blank = jnp.zeros((PX, 128), jnp.bfloat16)

    def project(h, mask, dst):
        for i in range(pairs):
            s = (me ^ mask) * per_owner + 2 * i
            both = jnp.concatenate([cells[h, block_ref[0, s]], cells[h, block_ref[0, s + 1]]], axis=1)
            grid = jnp.concatenate(
                [
                    jnp.concatenate([hot[s], blank], axis=1),
                    jnp.concatenate([blank, hot[s + 1]], axis=1),
                ],
                axis=0,
            )
            added = lax.dot_general(
                both, grid, (((1,), (1,)), ((), ())), preferred_element_type=jnp.float32
            )
            where = (h * devices + mask) * deep + 8 * i
            dst[pl.ds(pl.multiple_of(where, 8), 8), :] = added[:8] + added[8:]

    def rows_of(h, mask, count):
        return pl.ds(pl.multiple_of((h * devices + mask) * deep, 8), count * deep)

    def send_back(h, mask):
        these = rows_of(h, mask, 1)
        return remote(
            part.at[these], collected.at[these], back_sent, back_got.at[h], place(mask)
        )

    def project_part(h, g):
        low, high = part_of(g)

        @pl.loop(low, high, unroll=min(8, high - low))
        def _(mask):
            project(h, mask, part)

        @pl.loop(low, high)
        def _(mask):
            send_back(h, mask).start()

        if g == 0:
            project(h, 0, collected)

    def gather_up(h):
        arrived = collected.at[rows_of(h, 1, others)]
        remote(arrived, arrived, back_sent, back_got.at[h], place(1)).wait_recv()

        wide_left = lax.broadcasted_iota(jnp.int32, (tiles, 128), 1) < 64
        def column_of(k):
            came = jnp.concatenate(
                [
                    collected[pl.ds(h * devices * deep + 8 * i + k, devices, stride=deep), :]
                    for i in range(pairs)
                ],
                axis=0,
            )
            return jnp.concatenate(halves(jnp.concatenate([came, pltpu.roll(came, 64, 1)], axis=0)), axis=0)

        for k in range(0, 8, 2):
            both = jnp.dot(
                spread[...], jnp.concatenate([column_of(k), column_of(k + 1)], axis=1),
                preferred_element_type=jnp.float32,
            )
            for i in range(2):
                total = both[:, 128 * i : 128 * i + 128]
                image[pl.ds(h * tiles * 8 + k + i, tiles, stride=8), :] = jnp.where(
                    wide_left, total[:tiles], total[tiles:]
                )

        zero = jnp.zeros((8, 128), jnp.float32)

        def add(q, totals):
            these = pl.ds(pl.multiple_of(q * 128, 128), 128)
            tile = image[pl.ds(pl.multiple_of((h * tiles + q) * 8, 8), 8), :]
            image_ref[8 * h : 8 * h + 8, these] = tile
            way = way_ref[8 * h : 8 * h + 8, these]
            lean = lean_ref[8 * h : 8 * h + 8, these]
            scaled = jnp.broadcast_to(scale_ref[:, these], (8, 128)) * tile
            return totals[0] + way * tile, totals[1] + tile * lean, totals[2] + tile * scaled

        return [
            jnp.sum(total, axis=1, keepdims=True)
            for total in lax.fori_loop(0, tiles, add, (zero,) * 3, unroll=8)
        ]

    arrive(0)
    edges(0)
    edges_in(0)
    filter_all(0)
    for g in reversed(range(PARTS // 2, PARTS)):
        project_part(0, g)
    arrive(1)
    edges(1)
    for g in reversed(range(PARTS // 2)):
        project_part(0, g)
    edges_in(1)
    filter_all(1)
    for g in reversed(range(PARTS)):
        project_part(1, g)
    whole(ask_ref, 1, devices, ask_sent, ask_got).wait_send()
    for h in range(2):
        whole(served.at[h], 1, devices, sent, sent).wait_send()
    loads[3].wait()
    loads[4].wait()
    loads[8].wait()

    def lean_on(q, totals):
        these = pl.ds(pl.multiple_of(q * 128, 128), 128)
        scale = jnp.broadcast_to(scale_ref[:, these], (8, 128))
        made = []
        for h in range(2):
            old = old_ref[8 * h : 8 * h + 8, these]
            lean = scale * old
            lean_ref[8 * h : 8 * h + 8, these] = lean
            made.append(totals[h] + old * lean)
        return tuple(made)

    norms = [
        jnp.sum(total, axis=1, keepdims=True)
        for total in lax.fori_loop(0, tiles, lean_on, (jnp.zeros((8, 128), jnp.float32),) * 2, unroll=4)
    ]

    lanes = lax.broadcasted_iota(jnp.int32, (8, 128), 1)
    places = lax.broadcasted_iota(jnp.int32, (8, 128), 0)
    row = jnp.zeros((8, 128), jnp.float32)
    for h in range(2):
        for i, total in enumerate([norms[h]] + gather_up(h)):
            row = jnp.where(lanes == places * 8 + 4 * h + i, total, row)
    sums[...] = jnp.sum(row, axis=0, keepdims=True)

    def give_sums(mask):
        return remote(sums, held.at[mask], sum_sent, sum_got, place(mask))

    @functools.partial(partners)
    def _(mask):
        give_sums(mask).start()

    held[0] = sums[...]
    for h in range(2):
        these = part.at[rows_of(h, 1, others)]
        remote(these, these, back_sent, back_sent, place(1)).wait_send()
    whole(held, 1, devices, sum_sent, sum_got).wait()
    total = jnp.broadcast_to(jnp.sum(held[...], axis=0), (8, 128))
    for h in range(2):
        norm_old, curvature, cross, square = (
            jnp.take_along_axis(total, places * 8 + 4 * h + i, axis=1) for i in range(4)
        )
        step_size = norm_old / curvature
        norm_new = norm_old - step_size * (2.0 * cross - step_size * square)
        factor_ref[8 * h : 8 * h + 8, :] = jnp.where(lanes == 0, step_size, norm_new / norm_old)


def stay(array):
    return pltpu.with_memory_space_constraint(array, pltpu.HBM)


def one_step(diag, patch, at, way, old, scale, pixels, gains, band, groups, spans):
    devices = groups * spans
    rows = pixels.shape[0]
    blocks = patch.size
    pairs = blocks // devices // 2
    tiles = way.shape[1] // 128
    edge = (2, rows // 2, 8, 128)
    both = (2, devices, pairs, 8, 128)
    flat = (2 * devices * pairs * 8, 128)
    asks = (devices, 1, 128)
    dma = pltpu.SemaphoreType.DMA
    return pl.pallas_call(
        functools.partial(step_kernel, groups, spans),
        out_shape=(
            jax.ShapeDtypeStruct(way.shape, jnp.float32),
            jax.ShapeDtypeStruct((way.shape[0], 128), jnp.float32),
            jax.ShapeDtypeStruct(at.shape, jnp.float32),
        ),
        in_specs=[pl.BlockSpec(memory_space=pltpu.HBM)] * 9,
        out_specs=tuple(vmem(3)),
        scratch_shapes=[
            pltpu.SMEM(diag.shape, jnp.float32),
            pltpu.VMEM(patch.shape, jnp.int32),
            pltpu.VMEM(band.shape, jnp.float32),
            pltpu.VMEM(way.shape, jnp.float32),
            pltpu.VMEM(old.shape, jnp.float32),
            pltpu.VMEM(scale.shape, jnp.float32),
            pltpu.VMEM(pixels.shape, jnp.int32),
            pltpu.VMEM(gains.shape, jnp.float32),
            pltpu.SMEM((1, blocks), jnp.int32),
            pltpu.SMEM((1, blocks), jnp.int32),
            pltpu.VMEM((1, blocks), jnp.int32),
            pltpu.VMEM((1, blocks), jnp.int32),
            pltpu.VMEM(asks, jnp.int32),
            pltpu.SMEM(asks, jnp.int32),
            pltpu.VMEM(asks, jnp.int32),
            pltpu.VMEM((2, 2, tiles, 8, 128), jnp.float32),
            pltpu.VMEM(both, jnp.float32),
            pltpu.VMEM(both, jnp.float32),
            pltpu.VMEM((blocks, 128), jnp.int32),
            pltpu.VMEM((blocks, 128), jnp.int32),
            pltpu.VMEM((blocks, 128), jnp.float32),
            pltpu.VMEM((blocks, 128), jnp.float32),
            pltpu.VMEM((2, blocks, 8, 128), jnp.float32),
            pltpu.VMEM((rows, 256, 256), jnp.bfloat16),
            pltpu.VMEM((blocks, PX, 128), jnp.bfloat16),
            pltpu.VMEM(edge, jnp.float32),
            pltpu.VMEM(edge, jnp.float32),
            pltpu.VMEM(edge, jnp.float32),
            pltpu.VMEM(edge, jnp.float32),
            pltpu.VMEM((2, blocks, 16, 128), jnp.bfloat16),
            pltpu.VMEM(flat, jnp.float32),
            pltpu.VMEM(flat, jnp.float32),
            pltpu.VMEM((2 * tiles, 2 * blocks), jnp.bfloat16),
            pltpu.VMEM((2 * tiles * 8, 128), jnp.float32),
            pltpu.VMEM(way.shape, jnp.float32),
            pltpu.VMEM((1, 128), jnp.float32),
            pltpu.VMEM((devices, 1, 128), jnp.float32),
            dma((9,)),
            dma,
            dma,
            dma,
            dma((2,)),
            dma,
            dma((2, PARTS)),
            dma((2, 2)),
            dma((2, 2)),
            dma,
            dma((2,)),
            dma,
            dma,
        ],
        compiler_params=pltpu.CompilerParams(
            collective_id=0, has_side_effects=True, vmem_limit_bytes=32 * 1024 * 1024
        ),
    )(diag, patch, at, way, old, scale, pixels, gains, band)


def per_device(
    iterate, residual, direction, precond, patch_ids, pixel_in, weights, filter_diag, filter_band
):
    groups, spans = lax.axis_size("det"), lax.axis_size("tm")
    image_map, factor, kept = one_step(
        *map(stay, (filter_diag, patch_ids.T, iterate, direction, residual, precond[None, :])),
        *map(stay, (pixel_in, weights, filter_band)), groups, spans,
    )
    step_size, ratio = factor[:, 0:1], factor[:, 1:2]
    new_iterate = kept + step_size * direction
    new_residual = residual - step_size * image_map
    new_direction = precond * new_residual + ratio * direction
    return (new_iterate, new_residual, new_direction)


def solution(mesh):
    in_specs = (
        P(None, ("det", "tm")),
        P(None, ("det", "tm")),
        P(None, ("det", "tm")),
        P(("det", "tm")),
        P("det", "tm"),
        P("det", "tm"),
        P("det", "tm"),
        P("det"),
        P("det", None),
    )
    out_specs = (P(None, ("det", "tm")), P(None, ("det", "tm")), P(None, ("det", "tm")))
    return jax.shard_map(
        per_device, mesh=mesh, in_specs=in_specs, out_specs=out_specs, check_vma=False
    )
```

```python
import functools

import jax
import jax.numpy as jnp
from jax import lax
from jax.experimental import pallas as pl
from jax.experimental.pallas import tpu as pltpu
from jax.sharding import PartitionSpec as P

PX = 64
MESH = pl.DeviceIdType.MESH


def halves(values):
    top = values.astype(jnp.bfloat16)
    return top, (values - top.astype(jnp.float32)).astype(jnp.bfloat16)


PARTS = 8


def vmem(count):
    return [pl.BlockSpec(memory_space=pltpu.VMEM)] * count


def partners_of(groups, spans):
    group, span = lax.axis_index("det"), lax.axis_index("tm")
    me = group * spans + span
    shift = spans.bit_length() - 1

    def place(mask):
        return (group ^ (mask >> shift), span ^ (mask & (spans - 1)))

    return me, group, span, place


def remote(src, dst, sent, got, device):
    return pltpu.make_async_remote_copy(
        src_ref=src, dst_ref=dst, send_sem=sent, recv_sem=got, device_id=device, device_id_type=MESH
    )


def step_kernel(
    groups, spans,
    diag_hbm, patch_hbm, at_hbm, way_hbm, old_hbm, scale_hbm, pixel_hbm, gain_hbm, band_hbm,
    image_ref, factor_ref, at_ref,
    diag_ref, patch_ref, band_ref, way_ref, old_ref, scale_ref, pixel_ref, gain_ref,
    slot_ref, block_ref, slots, listed, ask_ref, numbers, asked, table, served, patches, pixels, turned, gains, turned_gains, line, bands, hot,
    head, tail, before, after, cells, part, collected, spread, image, lean_ref, sums, held,
    load_sem, ask_sent, ask_got, local, list_sem, sent, got, edge_sent, edge_got, back_sent, back_got,
    sum_sent, sum_got,
):
    devices = groups * spans
    me, group, span, place = partners_of(groups, spans)
    rows = pixel_ref.shape[0]
    blocks = block_ref.shape[1]
    per_row = blocks // rows
    per_owner = blocks // devices
    pairs = per_owner // 2
    half = rows // 2
    tiles = way_ref.shape[1] // 128
    deep = pairs * 8
    others = devices - 1
    width = devices // PARTS
    left = lax.broadcasted_iota(jnp.int32, (8, 128), 1) < 64

    loads = [
        pltpu.make_async_copy(src, dst, load_sem.at[i])
        for i, (src, dst) in enumerate(
            [(way_hbm, way_ref), (pixel_hbm, pixel_ref), (gain_hbm, gain_ref), (old_hbm, old_ref), (scale_hbm, scale_ref),
             (band_hbm, band_ref), (diag_hbm, diag_ref), (patch_hbm, patch_ref), (at_hbm, at_ref)]
        )
    ]
    barrier = pltpu.get_barrier_semaphore()

    def partners(run):
        @pl.loop(0, others)
        def _(n):
            run(others - n)

    @functools.partial(partners)
    def _(mask):
        pl.semaphore_signal(barrier, inc=1, device_id=place(mask), device_id_type=MESH)

    for i in (7, 0, 1, 2, 5, 6, 3, 4, 8):
        loads[i].start()

    lane8 = lax.broadcasted_iota(jnp.int32, (8, 128), 1)
    row8 = lax.broadcasted_iota(jnp.int32, (8, 128), 0)
    lane1 = lax.broadcasted_iota(jnp.int32, (1, 128), 1)
    square_row = lax.broadcasted_iota(jnp.int32, (128, 128), 0)
    square_lane = lax.broadcasted_iota(jnp.int32, (128, 128), 1)
    own_patches = 2 * tiles
    own_shift = own_patches.bit_length() - 1
    row_shift = rows.bit_length() - 1
    chunks = range(blocks // 128)

    def as_column(row):
        return jnp.broadcast_to(row, (128, 128)).T

    def down(values):
        return jnp.sum(values, axis=0, keepdims=True)

    loads[7].wait()
    padded = jnp.concatenate([patch_ref[...], jnp.zeros((per_row, 128 - rows), jnp.int32)], axis=1)
    repeated = jnp.take_along_axis(padded, lane8 & (rows - 1), axis=1)
    lies = [
        down(jnp.where(row8 == k * (128 // rows) + (lane8 >> row_shift), repeated, 0)) for k in chunks
    ]
    owners = [jnp.right_shift(lie, own_shift) for lie in lies]
    packed = [
        (((lane1 & (rows - 1)) * per_row + k * (128 // rows) + (lane1 >> row_shift)) << own_shift)
        + (lies[k] & (own_patches - 1))
        for k in chunks
    ]
    owner_columns = [as_column(owner) for owner in owners]
    packed_columns = [as_column(pack) for pack in packed]
    slot_rows = []
    for k in chunks:
        rank = jnp.zeros((128, 128), jnp.int32)
        for c in chunks:
            same = (owner_columns[c] == owners[k]) & (square_row + 128 * c < square_lane + 128 * k)
            rank = rank + jnp.where(same, 1, 0)
        slot_rows.append(owners[k] * per_owner + down(rank))
        slots[:, 128 * k : 128 * k + 128] = slot_rows[k] & (blocks - 1)
    slot_columns = [as_column(row) for row in slot_rows]
    for k in chunks:
        found = jnp.zeros((128, 128), jnp.int32)
        for c in chunks:
            found = found + jnp.where(slot_columns[c] == square_lane + 128 * k, packed_columns[c], 0)
        by_slot = down(found)
        listed[:, 128 * k : 128 * k + 128] = jnp.right_shift(by_slot, own_shift) & (blocks - 1)
        wide = jnp.broadcast_to(by_slot & (own_patches - 1), (8, 128))
        for p in range(128 // per_owner):
            turn = (128 - p * per_owner) % 128
            ask_ref[k * (128 // per_owner) + p] = (pltpu.roll(wide, turn, 1) if turn else wide)[:1]
    lists = [
        pltpu.make_async_copy(slots, slot_ref, list_sem.at[0]),
        pltpu.make_async_copy(listed, block_ref, list_sem.at[1]),
    ]
    for copy in lists:
        copy.start()
    asked[0] = ask_ref[me]
    pl.semaphore_wait(barrier, others)

    def ask(mask):
        return remote(ask_ref.at[me ^ mask], asked.at[mask], ask_sent, ask_got, place(mask))

    def give(h, mask):
        return remote(
            served.at[h, mask], patches.at[h, mask], sent, got.at[h, mask // width], place(mask)
        )

    def whole(ref, low, high, sent_sem, got_sem):
        these = ref.at[pl.ds(low, high - low)]
        return remote(these, these, sent_sem, got_sem, place(1))

    for mask in range(others, 0, -1):
        ask(mask).start()

    loads[0].wait()

    @pl.loop(0, tiles, unroll=2)
    def _(q):
        for h in range(2):
            tile = way_ref[8 * h : 8 * h + 8, pl.ds(pl.multiple_of(q * 128, 128), 128)]
            table[0, h, q] = tile
            table[1, h, q] = pltpu.roll(tile, 64, 1)

    whole(asked, 1, devices, ask_sent, ask_got).wait_recv()
    move = pltpu.make_async_copy(asked, numbers, local)
    move.start()
    move.wait()

    def serve(h, mask, dst):
        for i in range(pairs):
            a, b = numbers[mask, 0, 2 * i], numbers[mask, 0, 2 * i + 1]
            dst[h, mask, i] = jnp.where(left, table[a & 1, h, a >> 1], table[1 - (b & 1), h, b >> 1])

    def part_of(g):
        return max(1, g * width), (g + 1) * width

    def offer(h, g):
        low, high = part_of(g)

        @pl.loop(low, high)
        def _(mask):
            serve(h, mask, served)
            give(h, mask).start()

    for g in reversed(range(PARTS)):
        offer(0, g)
    for h in range(2):
        serve(h, 0, patches)

    loads[1].wait()
    loads[2].wait()
    for r in range(0, rows, 8):
        for j in range(per_row):
            these = pl.ds(r * per_row + j, 8, stride=per_row)
            pixel = pixel_ref[r : r + 8, 128 * j : 128 * j + 128]
            gain = gain_ref[r : r + 8, 128 * j : 128 * j + 128]
            pixels[these, :] = pixel
            turned[these, :] = pltpu.roll(pixel, 64, 1)
            gains[these, :] = gain
            turned_gains[these, :] = pltpu.roll(gain, 64, 1)

    for copy in lists:
        copy.wait()

    lane = lax.broadcasted_iota(jnp.int32, (1, 128), 1)
    loads[5].wait()
    loads[6].wait()
    band = jnp.concatenate([band_ref[...], jnp.zeros((rows, 128 - band_ref.shape[1]), jnp.float32)], axis=1)
    wanted = jnp.broadcast_to(jnp.where(lane < 64, 63 - lane, jnp.maximum(lane - 65, 0)), (rows, 128))
    upper = jnp.take_along_axis(band, wanted, axis=1)
    lower = jnp.where(
        lane == 0, jnp.take_along_axis(band, jnp.full((rows, 128), 63, jnp.int32), axis=1), 0.0
    )
    held_bands = jnp.concatenate([lower, upper], axis=1)

    wide_lane = lax.broadcasted_iota(jnp.int32, (1, 256), 1)
    for d in range(rows):
        base = jnp.where(wide_lane == 192, diag_ref[d], held_bands[d : d + 1])
        around = pltpu.roll(jnp.broadcast_to(base, (128, 256)), 0, 1, stride=1, stride_axis=0)
        bands[d] = jnp.concatenate(
            [
                jnp.concatenate(halves(around[:, :128]), axis=1),
                jnp.concatenate(halves(around[:, 128:]), axis=1),
            ],
            axis=0,
        )

    spot = lax.broadcasted_iota(jnp.int32, (PX, 128), 0)

    @pl.loop(0, blocks, unroll=2)
    def _(s):
        pixel = jnp.broadcast_to(pixels[pl.ds(block_ref[0, s], 1), :], (PX, 128))
        hot[s] = jnp.where(spot == pixel, 1.0, 0.0).astype(jnp.bfloat16)

    asks = asked[:, 0, :]
    even = jnp.concatenate(
        [jnp.broadcast_to(asks[:, 2 * i : 2 * i + 1], (devices, 2 * tiles)) for i in range(pairs)], axis=0
    )
    odd = jnp.concatenate(
        [jnp.broadcast_to(asks[:, 2 * i + 1 : 2 * i + 2], (devices, 2 * tiles)) for i in range(pairs)], axis=0
    )
    column = lax.broadcasted_iota(jnp.int32, even.shape, 1)
    first = column < tiles
    target = jnp.where(first, 2 * column, 2 * (column - tiles) + 1)
    straight = jnp.where(jnp.where(first, even, odd) == target, 1.0, 0.0)
    crossed = jnp.where(jnp.where(first, odd, even) == target, 1.0, 0.0)
    spread[...] = jnp.concatenate([straight.T, crossed.T] * 2, axis=1).astype(jnp.bfloat16)

    def scan(h, mask):
        for i in range(pairs):
            patch = patches[h, mask, i]
            for side in range(2):
                s = (me ^ mask) * per_owner + 2 * i + side
                b = block_ref[0, s]
                pixel = jnp.broadcast_to(turned[pl.ds(b, 1), :], (8, 128)) + 64 * side
                gain = jnp.broadcast_to(turned_gains[pl.ds(b, 1), :], (8, 128))
                line[h, s] = jnp.take_along_axis(patch, pixel, axis=1) * gain

    def arrive(h):
        scan(h, 0)
        for g in reversed(range(PARTS)):
            low, high = part_of(g)
            whole(patches.at[h], low, high, sent, got.at[h, g]).wait_recv()
            if h == 0 and PARTS // 2 <= g < PARTS - 1:
                offer(1, g + 1)
                if g == PARTS // 2:
                    offer(1, g)
                    for later in reversed(range(PARTS // 2)):
                        offer(1, later)

            @pl.loop(low, high, unroll=2)
            def _(mask):
                scan(h, mask)


    forth = [
        remote(tail.at[h], before.at[h], edge_sent.at[h, 0], edge_got.at[h, 0],
               (group, lax.rem(span + 1, spans)))
        for h in range(2)
    ]
    back = [
        remote(head.at[h], after.at[h], edge_sent.at[h, 1], edge_got.at[h, 1],
               (group, lax.rem(span + spans - 1, spans)))
        for h in range(2)
    ]

    def edges(h):
        @pl.loop(0, half)
        def _(d):
            start, end = d, d + (per_row - 1) * rows
            head[h, d] = jnp.where(
                left, pltpu.roll(line[h, slot_ref[0, start]], 64, 1), line[h, slot_ref[0, start + half]]
            )
            tail[h, d] = jnp.where(
                left, line[h, slot_ref[0, end]], pltpu.roll(line[h, slot_ref[0, end + half]], 64, 1)
            )

        forth[h].start()
        back[h].start()

    def edges_in(h):
        forth[h].wait()
        back[h].wait()

        @pl.when(span == 0)
        def _():
            before[h] = jnp.zeros_like(before[h])

        @pl.when(span == spans - 1)
        def _():
            after[h] = jnp.zeros_like(after[h])

    def one_row(h, d, early, late):
        mine = [early] + [line[h, slot_ref[0, j * rows + d]] for j in range(per_row)] + [late]
        shifted = [jnp.where(left, mine[m], mine[m + 1]) for m in range(per_row + 1)]
        near = jnp.concatenate(shifted[:-1], axis=0)
        far = jnp.concatenate(shifted[1:], axis=0)
        wide = jnp.concatenate(
            [jnp.concatenate(halves(near), axis=0), jnp.concatenate(halves(far), axis=0)], axis=1
        )
        made = jnp.dot(wide, bands[d], preferred_element_type=jnp.float32)
        n = 8 * per_row
        filtered = made[:n, :128] + (made[n:, :128] + made[:n, 128:])
        for j in range(per_row):
            gain = jnp.broadcast_to(gains[pl.ds(d * per_row + j, 1), :], (8, 128))
            values = filtered[8 * j : 8 * j + 8] * gain
            top = values.astype(jnp.bfloat16).astype(jnp.float32)
            cells[h, d * per_row + j] = jnp.concatenate([top, values - top], axis=0).astype(jnp.bfloat16)

    def filter_all(h):
        @pl.loop(0, half, unroll=2)
        def _(d):
            early, late = before[h, d], after[h, d]
            one_row(h, d, early, pltpu.roll(late, 64, 1))
            one_row(h, d + half, pltpu.roll(early, 64, 1), late)

    blank = jnp.zeros((PX, 128), jnp.bfloat16)

    def project(h, mask, dst):
        for i in range(pairs):
            s = (me ^ mask) * per_owner + 2 * i
            both = jnp.concatenate([cells[h, block_ref[0, s]], cells[h, block_ref[0, s + 1]]], axis=1)
            grid = jnp.concatenate(
                [
                    jnp.concatenate([hot[s], blank], axis=1),
                    jnp.concatenate([blank, hot[s + 1]], axis=1),
                ],
                axis=0,
            )
            added = lax.dot_general(
                both, grid, (((1,), (1,)), ((), ())), preferred_element_type=jnp.float32
            )
            where = (h * devices + mask) * deep + 8 * i
            dst[pl.ds(pl.multiple_of(where, 8), 8), :] = added[:8] + added[8:]

    def rows_of(h, mask, count):
        return pl.ds(pl.multiple_of((h * devices + mask) * deep, 8), count * deep)

    def send_back(h, mask):
        these = rows_of(h, mask, 1)
        return remote(
            part.at[these], collected.at[these], back_sent, back_got.at[h], place(mask)
        )

    def project_part(h, g):
        low, high = part_of(g)

        @pl.loop(low, high, unroll=min(8, high - low))
        def _(mask):
            project(h, mask, part)

        @pl.loop(low, high)
        def _(mask):
            send_back(h, mask).start()

        if g == 0:
            project(h, 0, collected)

    def gather_up(h):
        arrived = collected.at[rows_of(h, 1, others)]
        remote(arrived, arrived, back_sent, back_got.at[h], place(1)).wait_recv()

        wide_left = lax.broadcasted_iota(jnp.int32, (tiles, 128), 1) < 64
        def column_of(k):
            came = jnp.concatenate(
                [
                    collected[pl.ds(h * devices * deep + 8 * i + k, devices, stride=deep), :]
                    for i in range(pairs)
                ],
                axis=0,
            )
            return jnp.concatenate(halves(jnp.concatenate([came, pltpu.roll(came, 64, 1)], axis=0)), axis=0)

        for k in range(0, 8, 2):
            both = jnp.dot(
                spread[...], jnp.concatenate([column_of(k), column_of(k + 1)], axis=1),
                preferred_element_type=jnp.float32,
            )
            for i in range(2):
                total = both[:, 128 * i : 128 * i + 128]
                image[pl.ds(h * tiles * 8 + k + i, tiles, stride=8), :] = jnp.where(
                    wide_left, total[:tiles], total[tiles:]
                )

        zero = jnp.zeros((8, 128), jnp.float32)

        def add(q, totals):
            these = pl.ds(pl.multiple_of(q * 128, 128), 128)
            tile = image[pl.ds(pl.multiple_of((h * tiles + q) * 8, 8), 8), :]
            image_ref[8 * h : 8 * h + 8, these] = tile
            way = way_ref[8 * h : 8 * h + 8, these]
            lean = lean_ref[8 * h : 8 * h + 8, these]
            scaled = jnp.broadcast_to(scale_ref[:, these], (8, 128)) * tile
            return totals[0] + way * tile, totals[1] + tile * lean, totals[2] + tile * scaled

        return [
            jnp.sum(total, axis=1, keepdims=True)
            for total in lax.fori_loop(0, tiles, add, (zero,) * 3, unroll=8)
        ]

    arrive(0)
    edges(0)
    edges_in(0)
    filter_all(0)
    for g in reversed(range(PARTS // 2, PARTS)):
        project_part(0, g)
    arrive(1)
    edges(1)
    for g in reversed(range(PARTS // 2)):
        project_part(0, g)
    edges_in(1)
    filter_all(1)
    for g in reversed(range(PARTS)):
        project_part(1, g)
    whole(ask_ref, 1, devices, ask_sent, ask_got).wait_send()
    for h in range(2):
        whole(served.at[h], 1, devices, sent, sent).wait_send()
    loads[3].wait()
    loads[4].wait()
    loads[8].wait()

    def lean_on(q, totals):
        these = pl.ds(pl.multiple_of(q * 128, 128), 128)
        scale = jnp.broadcast_to(scale_ref[:, these], (8, 128))
        made = []
        for h in range(2):
            old = old_ref[8 * h : 8 * h + 8, these]
            lean = scale * old
            lean_ref[8 * h : 8 * h + 8, these] = lean
            made.append(totals[h] + old * lean)
        return tuple(made)

    norms = [
        jnp.sum(total, axis=1, keepdims=True)
        for total in lax.fori_loop(0, tiles, lean_on, (jnp.zeros((8, 128), jnp.float32),) * 2, unroll=4)
    ]

    lanes = lax.broadcasted_iota(jnp.int32, (8, 128), 1)
    places = lax.broadcasted_iota(jnp.int32, (8, 128), 0)
    row = jnp.zeros((8, 128), jnp.float32)
    for h in range(2):
        for i, total in enumerate([norms[h]] + gather_up(h)):
            row = jnp.where(lanes == places * 8 + 4 * h + i, total, row)
    sums[...] = jnp.sum(row, axis=0, keepdims=True)

    def give_sums(mask):
        return remote(sums, held.at[mask], sum_sent, sum_got, place(mask))

    for mask in range(others, 0, -1):
        give_sums(mask).start()

    held[0] = sums[...]
    for h in range(2):
        these = part.at[rows_of(h, 1, others)]
        remote(these, these, back_sent, back_sent, place(1)).wait_send()
    whole(held, 1, devices, sum_sent, sum_got).wait()
    total = jnp.broadcast_to(jnp.sum(held[...], axis=0), (8, 128))
    for h in range(2):
        norm_old, curvature, cross, square = (
            jnp.take_along_axis(total, places * 8 + 4 * h + i, axis=1) for i in range(4)
        )
        step_size = norm_old / curvature
        norm_new = norm_old - step_size * (2.0 * cross - step_size * square)
        factor_ref[8 * h : 8 * h + 8, :] = jnp.where(lanes == 0, step_size, norm_new / norm_old)


def stay(array):
    return pltpu.with_memory_space_constraint(array, pltpu.HBM)


def one_step(diag, patch, at, way, old, scale, pixels, gains, band, groups, spans):
    devices = groups * spans
    rows = pixels.shape[0]
    blocks = patch.size
    pairs = blocks // devices // 2
    tiles = way.shape[1] // 128
    edge = (2, rows // 2, 8, 128)
    both = (2, devices, pairs, 8, 128)
    flat = (2 * devices * pairs * 8, 128)
    asks = (devices, 1, 128)
    dma = pltpu.SemaphoreType.DMA
    return pl.pallas_call(
        functools.partial(step_kernel, groups, spans),
        out_shape=(
            jax.ShapeDtypeStruct(way.shape, jnp.float32),
            jax.ShapeDtypeStruct((way.shape[0], 128), jnp.float32),
            jax.ShapeDtypeStruct(at.shape, jnp.float32),
        ),
        in_specs=[pl.BlockSpec(memory_space=pltpu.HBM)] * 9,
        out_specs=tuple(vmem(3)),
        scratch_shapes=[
            pltpu.SMEM(diag.shape, jnp.float32),
            pltpu.VMEM(patch.shape, jnp.int32),
            pltpu.VMEM(band.shape, jnp.float32),
            pltpu.VMEM(way.shape, jnp.float32),
            pltpu.VMEM(old.shape, jnp.float32),
            pltpu.VMEM(scale.shape, jnp.float32),
            pltpu.VMEM(pixels.shape, jnp.int32),
            pltpu.VMEM(gains.shape, jnp.float32),
            pltpu.SMEM((1, blocks), jnp.int32),
            pltpu.SMEM((1, blocks), jnp.int32),
            pltpu.VMEM((1, blocks), jnp.int32),
            pltpu.VMEM((1, blocks), jnp.int32),
            pltpu.VMEM(asks, jnp.int32),
            pltpu.SMEM(asks, jnp.int32),
            pltpu.VMEM(asks, jnp.int32),
            pltpu.VMEM((2, 2, tiles, 8, 128), jnp.float32),
            pltpu.VMEM(both, jnp.float32),
            pltpu.VMEM(both, jnp.float32),
            pltpu.VMEM((blocks, 128), jnp.int32),
            pltpu.VMEM((blocks, 128), jnp.int32),
            pltpu.VMEM((blocks, 128), jnp.float32),
            pltpu.VMEM((blocks, 128), jnp.float32),
            pltpu.VMEM((2, blocks, 8, 128), jnp.float32),
            pltpu.VMEM((rows, 256, 256), jnp.bfloat16),
            pltpu.VMEM((blocks, PX, 128), jnp.bfloat16),
            pltpu.VMEM(edge, jnp.float32),
            pltpu.VMEM(edge, jnp.float32),
            pltpu.VMEM(edge, jnp.float32),
            pltpu.VMEM(edge, jnp.float32),
            pltpu.VMEM((2, blocks, 16, 128), jnp.bfloat16),
            pltpu.VMEM(flat, jnp.float32),
            pltpu.VMEM(flat, jnp.float32),
            pltpu.VMEM((2 * tiles, 2 * blocks), jnp.bfloat16),
            pltpu.VMEM((2 * tiles * 8, 128), jnp.float32),
            pltpu.VMEM(way.shape, jnp.float32),
            pltpu.VMEM((1, 128), jnp.float32),
            pltpu.VMEM((devices, 1, 128), jnp.float32),
            dma((9,)),
            dma,
            dma,
            dma,
            dma((2,)),
            dma,
            dma((2, PARTS)),
            dma((2, 2)),
            dma((2, 2)),
            dma,
            dma((2,)),
            dma,
            dma,
        ],
        compiler_params=pltpu.CompilerParams(
            collective_id=0, has_side_effects=True, vmem_limit_bytes=32 * 1024 * 1024
        ),
    )(diag, patch, at, way, old, scale, pixels, gains, band)


def per_device(
    iterate, residual, direction, precond, patch_ids, pixel_in, weights, filter_diag, filter_band
):
    groups, spans = lax.axis_size("det"), lax.axis_size("tm")
    image_map, factor, kept = one_step(
        *map(stay, (filter_diag, patch_ids.T, iterate, direction, residual, precond[None, :])),
        *map(stay, (pixel_in, weights, filter_band)), groups, spans,
    )
    step_size, ratio = factor[:, 0:1], factor[:, 1:2]
    new_iterate = kept + step_size * direction
    new_residual = residual - step_size * image_map
    new_direction = precond * new_residual + ratio * direction
    return (new_iterate, new_residual, new_direction)


def solution(mesh):
    in_specs = (
        P(None, ("det", "tm")),
        P(None, ("det", "tm")),
        P(None, ("det", "tm")),
        P(("det", "tm")),
        P("det", "tm"),
        P("det", "tm"),
        P("det", "tm"),
        P("det"),
        P("det", None),
    )
    out_specs = (P(None, ("det", "tm")), P(None, ("det", "tm")), P(None, ("det", "tm")))
    return jax.shard_map(
        per_device, mesh=mesh, in_specs=in_specs, out_specs=out_specs, check_vma=False
    )
```
